128 devices in a mesh: clip: 8 (over y_hi, x), tok: 16 (over z, y_lo, core).
Axes of the slice: x: 4, y: 4 (y_hi: 2, y_lo: 2; y = y_hi * 2 + y_lo), z: 4, core: 2. Of those that a mesh axis runs over, the one named last changes fastest.
Arguments:
- features: bfloat16 [2, 20480, 1408], P(None, ('clip', 'tok')), may hold values from -6 to 6
- masked_index: int32 [128, 1408], P(('clip', 'tok')), may hold values from 0 to 1567, as said below
- pos_table: bfloat16 [1568, 512], replicated, may hold values from -6 to 6
- mask_token: bfloat16 [512], replicated, may hold values from -6 to 6
- key_gain: bfloat16 [2, 1408], replicated, may hold values from 0.5 to 1.5
- key_weight: bfloat16 [2, 1408, 1024], replicated, may hold values from -0.15625 to 0.15625
- query_gain: bfloat16 [2, 512], replicated, may hold values from 0.5 to 1.5
- query_weight: bfloat16 [2, 512, 512], replicated, may hold values from -0.25 to 0.25
- out_weight: bfloat16 [2, 512, 512], replicated, may hold values from -0.25 to 0.25
- out_gain: bfloat16 [512], replicated, may hold values from 0.5 to 1.5
- head_weight: bfloat16 [512, 1536], replicated, may hold values from -0.25 to 0.25
- target: bfloat16 [128, 1408, 1536], P(('clip', 'tok')), may hold values from -12 to 12
Outputs:
- loss: float32 [], replicated
- feature_grad: bfloat16 [2, 20480, 1408], P(None, ('clip', 'tok'))
- key_grad: float32 [2, 1408, 1024], P(None, ('clip', 'tok'))
- query_grad: float32 [2, 512, 512], P(None, ('clip', 'tok'))
- out_grad: float32 [2, 512, 512], P(None, ('clip', 'tok'))
- head_grad: float32 [512, 1536], P(('clip', 'tok'))
The draws below stay inside these ranges and needn't reach their ends.
Inputs may be any that keep to these rules, and one draw needn't show every extreme that they name: `masked_index`: each row lists, increasing, the positions f * 196 + s of one clip's masked tokens: the same 196 - 20 patch positions s in each of the 8 time positions f.
All inputs are finite; a program needn't handle non-finite values.
Results may differ from the reference program's by a relative error of at most 0.013.
Values sent between devices are 32-bit elements; how exact they have to be, the bound alone decides.
A program may use at most 256 MiB of HBM per device.

```python
import math
import jax
import jax.numpy as jnp
from jax import lax

D = 1408
DD = 512
HEADS = 16
PIX = 1536
FRAMES = 8
SPATIAL = 196
KEEP = 20
LAYERS = 2
VIS = 160
MASKED = 1408
TOKS = 1568
CLIPS = 128


def draw_masked_index(key, part):
    key = jax.random.fold_in(key, 11)

    def one_clip(clip_key):
        shuffled = jax.random.permutation(clip_key, SPATIAL - 2).astype(jnp.int32) + 1
        first = jnp.zeros((1,), jnp.int32)
        last = jnp.full((1,), SPATIAL - 1, jnp.int32)
        masked = jnp.sort(jnp.concatenate([first, shuffled[KEEP:], last]))
        frames = jnp.arange(FRAMES, dtype=jnp.int32)[:, None] * SPATIAL + masked[None, :].astype(jnp.int32)
        return frames.reshape(-1).astype(jnp.int32)
    clip_keys = jax.random.split(key, CLIPS)
    return jax.vmap(one_clip)(clip_keys)


def rising_scale(top_scale):
    place = jnp.arange(CLIPS, dtype=jnp.float32) / max(CLIPS - 1, 1)
    return (top_scale ** place)[:, None, None]


def draw_target(key, part):
    key = jax.random.fold_in(key, 13)
    noise = jax.random.truncated_normal(key, -6.0, 6.0, (CLIPS, MASKED, PIX), jnp.float32)
    values = noise * rising_scale(2.0)
    return values.astype(jnp.bfloat16)


def block_scale(key, shape, cuts, low, top_value):
    def one(dim, parts):
        steps = jax.random.uniform(jax.random.fold_in(jax.random.fold_in(key, 6), dim), (parts,), jnp.float32, low / len(cuts), top_value / len(cuts))
        return jnp.repeat(jnp.exp(steps), shape[dim] // parts).reshape((-1,) + (1,) * (len(shape) - dim - 1))

    loudness = one(*cuts[0])
    for cut in cuts[1:]:
        loudness = loudness * one(*cut)
    return loudness


def bell_draw(own_key, shape, scale, reach, cuts=(), kind=jnp.bfloat16):
    drawn = jax.random.normal(own_key, shape, jnp.float32) * scale
    if len(cuts) > 0:
        drawn = block_scale(own_key, shape, cuts, -0.22, 0.18) * drawn
    return jnp.clip(drawn, min=-reach, max=reach).astype(kind)


def setup_inputs(seed: int = 0) -> dict:
    streams_of = jax.random.split(jax.random.key(seed), 13)
    return {
        "features": bell_draw(streams_of[0], (LAYERS, CLIPS * VIS, D), 1.0, 6.0, ((1, 128),)),
        "masked_index": draw_masked_index(jax.random.fold_in(streams_of[12], 71), 0),
        "pos_table": bell_draw(streams_of[2], (TOKS, DD), 1.0, 6.0),
        "mask_token": bell_draw(streams_of[3], (DD,), 1.0, 6.0),
        "key_gain": jnp.clip(1.0 + 0.1 * jax.random.normal(streams_of[4], (LAYERS, D), jnp.float32), 0.5, 1.5).astype(jnp.bfloat16),
        "key_weight": bell_draw(streams_of[5], (LAYERS, D, 2 * DD), D ** -0.5, 0.15625),
        "query_gain": jnp.clip(1.0 + 0.1 * jax.random.normal(streams_of[6], (LAYERS, DD), jnp.float32), 0.5, 1.5).astype(jnp.bfloat16),
        "query_weight": bell_draw(streams_of[7], (LAYERS, DD, DD), DD ** -0.5, 0.25),
        "out_weight": bell_draw(streams_of[8], (LAYERS, DD, DD), DD ** -0.5, 0.25),
        "out_gain": jnp.clip(1.0 + 0.1 * jax.random.normal(streams_of[9], (DD,), jnp.float32), 0.5, 1.5).astype(jnp.bfloat16),
        "head_weight": bell_draw(streams_of[10], (DD, PIX), DD ** -0.5, 0.25),
        "target": draw_target(jax.random.fold_in(streams_of[12], 71), 0),
    }


EPSILON = 1e-06

def normalize(values, scale_gain):
    values = values.astype(jnp.float32)
    center = values - lax.optimization_barrier(jnp.mean(values, axis=-1, keepdims=True))
    spread = lax.optimization_barrier(jnp.mean(center * center, axis=-1, keepdims=True))
    return center * lax.rsqrt(spread + EPSILON) * scale_gain.astype(jnp.float32)

def round_twice(values):
    return lax.optimization_barrier(values.astype(jnp.bfloat16)).astype(jnp.float32)

def project_features(feature_rows, scale_gain, weight):
    normed = normalize(feature_rows, scale_gain).astype(jnp.bfloat16)
    return jnp.dot(normed, weight, preferred_element_type=jnp.float32)

def start_stream(positions, pos_table, mask_token):
    return mask_token.astype(jnp.float32) + pos_table[positions].astype(jnp.float32)

def attend(stream, key_values, scale_gain, query_weight, out_weight, query_probe, out_probe):
    clips, rows, width = stream.shape
    visible = key_values.shape[1]
    head_size = width // HEADS
    normed = normalize(stream, scale_gain).astype(jnp.bfloat16).reshape(clips * rows, width)
    queries = jnp.dot(normed, query_weight, preferred_element_type=jnp.float32) + query_probe
    queries = round_twice(queries).reshape(clips, rows, HEADS, head_size)
    keys = key_values[:, :, :width].reshape(clips, visible, HEADS, head_size)
    values = key_values[:, :, width:].reshape(clips, visible, HEADS, head_size)
    scores = jnp.einsum('crhe,cvhe->chrv', queries, keys, precision=lax.Precision.HIGHEST) / math.sqrt(head_size)
    probs = round_twice(jax.nn.softmax(scores, axis=-1))
    mixed = jnp.einsum('chrv,cvhe->crhe', probs, values, precision=lax.Precision.HIGHEST)
    mixed = mixed.astype(jnp.bfloat16).reshape(clips * rows, width)
    update = jnp.dot(mixed, out_weight, preferred_element_type=jnp.float32) + out_probe
    return (stream + update.reshape(clips, rows, width), (normed, mixed))

def decode(stream, key_values, query_gain, query_weight, out_weight, probes):
    saved = []
    for which_layer in range(len(key_values)):
        stream, kept = attend(stream, key_values[which_layer], query_gain[which_layer], query_weight[which_layer], out_weight[which_layer], probes[2 * which_layer], probes[2 * which_layer + 1])
        saved.append(kept)
    return (stream, saved)

def head_energy(stream, out_gain, head_weight, target, head_probe):
    width = stream.shape[-1]
    normed = normalize(stream, out_gain).astype(jnp.bfloat16).reshape(-1, width)
    predicted = jnp.dot(normed, head_weight, preferred_element_type=jnp.float32) + head_probe
    error = predicted - target.astype(jnp.float32).reshape(predicted.shape)
    squared = jnp.sum(error * error)
    return (0.5 * squared, (squared, normed))

def outer_sum(normed, cotangent):
    return lax.dot_general(normed, cotangent.astype(jnp.bfloat16), (((0,), (0,)), ((), ())), preferred_element_type=jnp.float32)

def reference(features, masked_index, pos_table, mask_token, key_gain, key_weight, query_gain, query_weight, out_weight, out_gain, head_weight, target):
    layers = features.shape[0]
    width = mask_token.shape[0]
    per_clip = features.reshape(layers, CLIPS, VIS, D).transpose(1, 0, 2, 3)

    def one_clip(carry, inputs):
        clip_features, positions, clip_target = inputs
        stream = start_stream(positions[None], pos_table, mask_token)
        rows = positions.shape[0]
        probes = tuple((jnp.zeros((rows, width), jnp.float32) for which in range(2 * layers)))
        kv_probes = tuple((jnp.zeros((VIS, 2 * width), jnp.float32) for which in range(layers)))
        head_probe = jnp.zeros((rows, head_weight.shape[1]), jnp.float32)

        def energy(clip_features, probes, kv_probes, head_probe):
            key_values = tuple((round_twice(project_features(clip_features[which_layer], key_gain[which_layer], key_weight[which_layer]) + kv_probes[which_layer])[None] for which_layer in range(layers)))
            final, saved = decode(stream, key_values, query_gain, query_weight, out_weight, probes)
            half_energy, (squared, head_normed) = head_energy(final, out_gain, head_weight, clip_target[None], head_probe)
            return (half_energy, (squared, saved, head_normed))
        unused, backward, (squared, saved, head_normed) = jax.vjp(energy, clip_features, probes, kv_probes, head_probe, has_aux=True)
        feature_grad, probe_grads, kv_grads, head_cotangent = backward(jnp.float32(1.0))
        key_part = jnp.stack([outer_sum(normalize(clip_features[which_layer], key_gain[which_layer]).astype(jnp.bfloat16), kv_grads[which_layer]) for which_layer in range(layers)])
        query_part = jnp.stack([outer_sum(saved[which_layer][0], probe_grads[2 * which_layer]) for which_layer in range(layers)])
        out_part = jnp.stack([outer_sum(saved[which_layer][1], probe_grads[2 * which_layer + 1]) for which_layer in range(layers)])
        head_part = outer_sum(head_normed, head_cotangent)
        total_squared, total_key, total_query, total_out, total_head = carry
        return ((total_squared + squared, total_key + key_part, total_query + query_part, total_out + out_part, total_head + head_part), feature_grad)
    start = (jnp.zeros((), jnp.float32), jnp.zeros((layers, D, 2 * width), jnp.float32), jnp.zeros((layers, width, width), jnp.float32), jnp.zeros((layers, width, width), jnp.float32), jnp.zeros(head_weight.shape, jnp.float32))
    totals, feature_grads = lax.scan(one_clip, start, (per_clip, masked_index, target))
    loss = totals[0] / (CLIPS * MASKED * PIX)
    feature_grad = feature_grads.transpose(1, 0, 2, 3).reshape(layers, CLIPS * VIS, D)
    return (loss, feature_grad, totals[1], totals[2], totals[3], totals[4])
```

```python
import math

import jax
import jax.numpy as jnp
from jax import lax
from jax.experimental import pallas as pl
from jax.experimental.pallas import tpu as pltpu
from jax.sharding import PartitionSpec as P

HEADS = 16
HS = 32
VIS = 160
D = 1408
DD = 512
PIX = 1536
ROWS = 1408
TOKS = 1568
CH = 256
EXT = 48
EPS = 1e-6
F32 = jnp.float32
BF = jnp.bfloat16
SCALE = 1.0 / math.sqrt(HS)
LOG2 = SCALE * math.log2(math.e)
GF = 4
GB = 2
SLOT = 3072


def nn(a, b):
    return lax.dot_general(a, b, (((1,), (0,)), ((), ())), preferred_element_type=F32)


def nt(a, b):
    return lax.dot_general(a, b, (((1,), (1,)), ((), ())), preferred_element_type=F32)


def wide(g, w):
    return jnp.concatenate([g] * (w // 128), axis=1)


def compute_kernel(
    idx_ref, feat_ref, tok_ref, kgain_ref, qgain_ref, ogain_ref,
    pos_hbm, kw_hbm, qw_hbm, ow_hbm, hw_hbm, tgt_hbm,
    loss_ref, fgrad_ref, g_hbm,
    pos, kw, qw, ow, hw, err, posT, qwT, owT, nf, nfT, k2, vx, vTx, kT, probs0, probs1,
    nq, qs, ms, dus, dqs, no, rs, invs, dx_all, dkvT, gains, q2, dme, stage, esum, sems, gsem,
):
    loads = [
        pltpu.make_async_copy(pos_hbm, pos, sems.at[0]),
        pltpu.make_async_copy(kw_hbm, kw, sems.at[1]),
        pltpu.make_async_copy(qw_hbm, qw, sems.at[2]),
        pltpu.make_async_copy(ow_hbm, ow, sems.at[3]),
        pltpu.make_async_copy(hw_hbm, hw, sems.at[4]),
        pltpu.make_async_copy(tgt_hbm.at[0], err, sems.at[5]),
    ]
    for i in (2, 3, 0, 1, 4, 5):
        loads[i].start()

    for i, row in enumerate((qgain_ref[0:1, :], qgain_ref[1:2, :], ogain_ref[...], tok_ref[...])):
        gains[i] = jnp.broadcast_to(row.astype(F32).reshape(1, DD), (128, DD)).T

    def feature_norm(l):
        f = feat_ref[l].astype(F32)
        c = f - jnp.mean(f, axis=1, keepdims=True)
        r = lax.rsqrt(jnp.mean(c * c, axis=1, keepdims=True) + EPS)
        return c * r, r

    for l in range(2):
        n = (feature_norm(l)[0] * kgain_ref[l:l + 1, :].astype(F32)).astype(BF)
        nf[l] = n
        nfT[l] = n.T
    loads[2].wait()
    loads[3].wait()
    for l in range(2):
        qwT[l] = qw[l].T
        owT[l] = ow[l].T
    loads[0].wait()
    posT[...] = pos[...].T
    loads[1].wait()
    tail = jnp.concatenate([jnp.ones((1, VIS), BF), jnp.zeros((EXT - HS - 1, VIS), BF)], axis=0)
    vtail = jnp.concatenate([jnp.ones((VIS, 2), BF), jnp.zeros((VIS, EXT - HS - 2), BF)], axis=1)
    for l in range(2):
        keys = nn(nf[l], kw[l, :, 0:DD]).astype(BF)
        vals = nn(nf[l], kw[l, :, DD:2 * DD]).astype(BF)
        kT[l] = keys.T
        vT = vals.T
        for h in range(HEADS):
            hs = slice(h * HS, (h + 1) * HS)
            k2[l, h] = jnp.concatenate([keys[:, hs], keys[:, hs]], axis=1)
            vx[l, h] = jnp.concatenate([vals[:, hs], vtail], axis=1)
            vTx[l, h] = jnp.concatenate([vT[hs, :], tail], axis=0)
    dkvT[...] = jnp.zeros_like(dkvT)
    esum[...] = jnp.zeros_like(esum)

    def norm(x, gain):
        c = x - jnp.mean(x, axis=0, keepdims=True)
        r = lax.rsqrt(jnp.mean(c * c, axis=0, keepdims=True) + EPS)
        return (c * r * gain).astype(BF), r

    def norm_back(dy, n, r, gain):
        n = n.astype(F32)
        m2 = jnp.mean(dy * n, axis=0, keepdims=True)
        dxh = dy * gain
        m1 = jnp.mean(dxh, axis=0, keepdims=True)
        return r * (dxh - m1 - n * (m2 / gain))

    def fwd_layer(l, x, t0, w):
        tsl = pl.ds(t0, w)
        n, r = norm(x, wide(gains[l], w))
        nq[l, :, tsl] = n
        rs[l, :, tsl] = r
        qb = nn(qwT[l], n).astype(BF)
        qs[l, :, tsl] = qb
        qf = qb.astype(F32) * LOG2
        hi = qf.astype(BF)
        lo = (qf - hi.astype(F32)).astype(BF)
        q2[:, 0:HS, 0:w] = hi.reshape(HEADS, HS, w)
        q2[:, HS:2 * HS, 0:w] = lo.reshape(HEADS, HS, w)

        def scores(h):
            return nn(k2[l, h], q2[h, :, 0:w])

        def soft(h, s):
            p = jnp.exp2(s - jnp.max(s, axis=0, keepdims=True)).astype(BF)
            if l == 0:
                probs0[h, :, tsl] = p
            else:
                probs1[h, :, 0:w] = p
            return p

        def mix(h, p):
            o = nn(vTx[l, h], p)
            inv = 1.0 / o[HS:HS + 1]
            invs[l, h:h + 1, tsl] = inv
            ms[l, h * HS:(h + 1) * HS, tsl] = (o[:HS] * inv).astype(BF)

        n_g = HEADS // GF
        s = [scores(u) for u in range(GF)]
        before = None
        for g in range(n_g):
            s2 = [scores((g + 1) * GF + u) for u in range(GF)] if g + 1 < n_g else None
            ps = [soft(g * GF + u, s[u]) for u in range(GF)]
            if before is not None:
                for u in range(GF):
                    mix((g - 1) * GF + u, before[u])
            s, before = s2, ps
        for u in range(GF):
            mix((n_g - 1) * GF + u, before[u])
        return x + nn(owT[l], ms[l, :, tsl])

    def bwd_layer(l, dx, t0, w):
        tsl = pl.ds(t0, w)
        du = dx.astype(BF)
        dus[:, tsl] = du
        dm = nn(ow[l], du).reshape(HEADS, HS, w) * invs[l, :, tsl].reshape(HEADS, 1, w)
        dm = dm.astype(BF)
        dme[:, 0:HS, 0:w] = dm
        dsum = jnp.sum(dm.astype(F32) * ms[l, :, tsl].astype(F32).reshape(HEADS, HS, w), axis=1, keepdims=True)
        hi = dsum.astype(BF)
        lo = (dsum - hi.astype(F32)).astype(BF)
        dme[:, HS:EXT, 0:w] = jnp.concatenate([-hi, -lo, jnp.zeros((HEADS, EXT - HS - 2, w), BF)], axis=1)

        def probs(h):
            return probs0[h, :, tsl] if l == 0 else probs1[h, :, 0:w]

        def dprobs(h):
            return nn(vx[l, h], dme[h, :, 0:w])

        def dscores(h, x):
            return (probs(h).astype(F32) * x).astype(BF)

        def rest(h, ds):
            hs = slice(h * HS, (h + 1) * HS)
            vs = slice(DD + h * HS, DD + (h + 1) * HS)
            dqs[hs, tsl] = (nn(kT[l, hs, :], ds) * SCALE).astype(BF)
            dkvT[l, hs, :] += nt(qs[l, hs, tsl], ds)
            dkvT[l, vs, :] += nt(dme[h, 0:HS, 0:w], probs(h))

        n_g = HEADS // GB
        x = [dprobs(u) for u in range(GB)]
        before = None
        for g in range(n_g):
            x2 = [dprobs((g + 1) * GB + u) for u in range(GB)] if g + 1 < n_g else None
            ds = [dscores(g * GB + u, x[u]) for u in range(GB)]
            if before is not None:
                for u in range(GB):
                    rest((g - 1) * GB + u, before[u])
            x, before = x2, ds
        for u in range(GB):
            rest((n_g - 1) * GB + u, before[u])

        dn = nn(qw[l], dqs[:, tsl])
        return dx + norm_back(dn, nq[l, :, tsl], rs[l, :, tsl], wide(gains[l], w))

    def chunk_a(t0, w):
        tsl = pl.ds(t0, w)
        ids = idx_ref[:, tsl]
        onehot = (lax.broadcasted_iota(jnp.int32, (TOKS, w), 0) == ids).astype(BF)
        x = wide(gains[3], w) + nn(posT[...], onehot)
        x = fwd_layer(0, x, t0, w)
        x = fwd_layer(1, x, t0, w)
        n, r = norm(x, wide(gains[2], w))
        no[:, tsl] = n
        nT = n.T
        e = nn(nT, hw[...]) - err[tsl, :].astype(F32)
        esum[...] += jnp.sum(e * e, axis=0, keepdims=True)
        eb = e.astype(BF)
        err[tsl, :] = eb
        dn = nt(hw[...], eb)
        dx = norm_back(dn, n, r, wide(gains[2], w))
        dx_all[:, tsl] = bwd_layer(1, dx, t0, w)

    def chunk_b(t0, w):
        tsl = pl.ds(t0, w)
        bwd_layer(0, dx_all[:, tsl], t0, w)

    loads[4].wait()
    loads[5].wait()
    full = ROWS // CH
    rem = ROWS - full * CH

    @pl.loop(0, full)
    def _(i):
        chunk_a(pl.multiple_of(i * CH, CH), CH)

    chunk_a(full * CH, rem)

    loss_ref[...] = jnp.full((8, 128), jnp.sum(esum[...]), F32)

    pending = [[], []]
    count = [0]

    def emit(dot, lhs, rhs, rows, width, share, dsts):
        slot = count[0] % 2
        count[0] += 1
        for cp in pending[slot]:
            cp.wait()
        parts = width // 128
        for c in range(width // 256):
            block = dot(lhs, rhs(c * 256))
            for j in range(2):
                stage[slot, pl.ds(2 * c + j, rows, stride=parts), :] = block[:, j * 128:(j + 1) * 128]
        n = rows * parts
        src = stage.at[slot, pl.ds(0, n)].reshape(n // share, share, 128)
        pending[slot] = []
        for i, (lo, hi, dst) in enumerate(dsts):
            cp = pltpu.make_async_copy(src.at[:, pl.ds(lo, hi - lo)], dst, gsem.at[slot, i])
            cp.start()
            pending[slot].append(cp)

    def grads_layer(l):
        emit(nt, nq[l], lambda c: dqs[c:c + 256, :], DD, DD, 16, [(0, 16, g_hbm.at[2, :, pl.ds(16 * l, 16)])])
        emit(nt, ms[l], lambda c: dus[c:c + 256, :], DD, DD, 16, [(0, 16, g_hbm.at[2, :, pl.ds(32 + 16 * l, 16)])])
        dkvT[l, 0:DD, :] = dkvT[l, 0:DD, :] * SCALE
        dT = dkvT[l].astype(BF)
        for b in range(4):
            emit(nt, nfT[l, b * 352:(b + 1) * 352, :], lambda c: dT[c:c + 256, :], 352, 2 * DD, 88,
                 [(0, 88, g_hbm.at[l, pl.ds(32 * b, 32), pl.ds(0, 88)])])
        d = dkvT[l].T.astype(BF)
        dn = nt(d, kw[l])
        xh, r = feature_norm(l)
        dxh = dn * kgain_ref[l:l + 1, :].astype(F32)
        m1 = jnp.mean(dxh, axis=1, keepdims=True)
        m2 = jnp.mean(dxh * xh, axis=1, keepdims=True)
        fgrad_ref[l] = (r * (dxh - m1 - xh * m2)).astype(BF)

    for b in range(2):
        to = pl.ds(64 * b, 64)
        emit(nn, no[b * 256:(b + 1) * 256, :], lambda c: err[:, c:c + 256], 256, PIX, 48, [
            (0, 8, g_hbm.at[0, to, pl.ds(88, 8)]),
            (8, 16, g_hbm.at[1, to, pl.ds(88, 8)]),
            (16, 48, g_hbm.at[2, to, pl.ds(64, 32)])])
    grads_layer(1)

    @pl.loop(0, full)
    def _(i):
        chunk_b(pl.multiple_of(i * CH, CH), CH)

    chunk_b(full * CH, rem)
    grads_layer(0)
    for cp in pending[0] + pending[1]:
        cp.wait()


def compute(features, masked_index, pos_table, mask_token, key_gain, key_weight, query_gain,
            query_weight, out_weight, out_gain, head_weight, target):
    vm = pl.BlockSpec(memory_space=pltpu.VMEM)
    hb = pl.BlockSpec(memory_space=pl.ANY)
    out_shape = (
        jax.ShapeDtypeStruct((8, 128), F32),
        jax.ShapeDtypeStruct((2, VIS, D), BF),
        jax.ShapeDtypeStruct((3, 128, 96, 128), F32),
    )
    V = pltpu.VMEM
    scratch = [
        V((TOKS, DD), BF), V((2, D, 2 * DD), BF), V((2, DD, DD), BF), V((2, DD, DD), BF), V((DD, PIX), BF),
        V((ROWS, PIX), BF), V((DD, TOKS), BF), V((2, DD, DD), BF), V((2, DD, DD), BF),
        V((2, VIS, D), BF), V((2, D, VIS), BF),
        V((2, HEADS, VIS, 2 * HS), BF), V((2, HEADS, VIS, EXT), BF), V((2, HEADS, EXT, VIS), BF), V((2, DD, VIS), BF),
        V((HEADS, VIS, ROWS), BF), V((HEADS, VIS, CH), BF),
        V((2, DD, ROWS), BF), V((2, DD, ROWS), BF), V((2, DD, ROWS), BF), V((DD, ROWS), BF), V((DD, ROWS), BF),
        V((DD, ROWS), BF), V((2, 1, ROWS), F32), V((2, HEADS, ROWS), F32), V((DD, ROWS), F32), V((2, 2 * DD, VIS), F32),
        V((4, DD, 128), F32), V((HEADS, 2 * HS, CH), BF), V((HEADS, EXT, CH), BF),
        V((2, SLOT, 128), F32), V((1, PIX), F32),
        pltpu.SemaphoreType.DMA((6,)), pltpu.SemaphoreType.DMA((2, 3)),
    ]
    return pl.pallas_call(
        compute_kernel,
        out_shape=out_shape,
        in_specs=[vm] * 6 + [hb] * 6,
        out_specs=[vm, vm, hb],
        scratch_shapes=scratch,
        compiler_params=pltpu.CompilerParams(vmem_limit_bytes=63 * 1024 * 1024),
        name="decode",
    )(
        masked_index, features, mask_token.reshape(1, DD), key_gain, query_gain, out_gain.reshape(1, DD),
        pos_table, key_weight, query_weight, out_weight, head_weight, target,
    )


MESH = pl.DeviceIdType.MESH
PARTS = 3
PROWS = 96
ORDERS = (("x", "y", "z"), ("y", "z", "x"), ("z", "x", "y"))


def part_index(coords):
    y = coords["y"]
    if isinstance(y, slice):
        return (y, coords["x"], coords["z"], y)
    return (y // 2, coords["x"], coords["z"], y % 2)


def block_shape(free):
    shape = []
    for name, size in (("y", 2), ("x", 4), ("z", 4), ("y", 2)):
        if name in free:
            shape.append(size)
    return tuple(shape)


def reduce_kernel(g_ref, loss_ref, k_out, q_out, o_out, h_out, l_out, own, got, lbuf, *rest):
    n_stage = 9
    first = rest[0:n_stage]
    second = rest[n_stage:2 * n_stage]
    send, recv, lsem = rest[2 * n_stage:]
    clip, tok = lax.axis_index("clip"), lax.axis_index("tok")
    me = {"x": clip % 4, "y": (clip // 4) * 2 + (tok // 2) % 2, "z": tok // 4}
    core = tok % 2

    def device(c, k):
        return ((c["y"] // 2) * 4 + c["x"], c["z"] * 4 + (c["y"] % 2) * 2 + k)

    def shifted(axis, by):
        c = dict(me)
        c[axis] = (me[axis] + by + 4) % 4
        return c

    partner = device(me, 1 - core)
    sides = {a: (device(shifted(a, 1), core), device(shifted(a, -1), core)) for a in "xyz"}

    barrier = pltpu.get_barrier_semaphore()
    for dev in [partner] + [d for a in "xyz" for d in sides[a]]:
        pl.semaphore_signal(barrier, inc=1, device_id=dev, device_id_type=MESH)
    pl.semaphore_wait(barrier, 7)

    counter = [0]

    def remote(src, dst, dev):
        i = counter[0]
        counter[0] += 1
        cp = pltpu.make_async_remote_copy(
            src_ref=src, dst_ref=dst, send_sem=send.at[i], recv_sem=recv.at[i], device_id=dev, device_id_type=MESH)
        cp.start()
        return cp

    full = slice(None)

    def coords_of(part, stage, j):
        c = {}
        for s, a in enumerate(ORDERS[part]):
            c[a] = me[a] if s < stage else (j if s == stage else full)
        return c

    def each(part, stage, body):
        free = [a for s, a in enumerate(ORDERS[part]) if s > stage]

        @pl.loop(0, 4 ** len(free))
        def _(i):
            c = {}
            for a in free:
                c[a] = i % 4
                i = i // 4
            body(c)

    def pick(part, stage, j, c):
        at = coords_of(part, stage, j)
        at.update(c)
        return (part,) + part_index(at)

    def place(part, stage, c):
        free = [a for s, a in enumerate(ORDERS[part]) if s > stage]
        out = []
        for name in ("yh", "x", "z", "yl"):
            if name[0] in free:
                out.append(c["y"] // 2 if name == "yh" else c["y"] % 2 if name == "yl" else c[name])
        return tuple(out)

    mine, swaps = {}, {}
    k = 0
    for by in (2, 1, 3, 0):
        for part in range(PARTS):
            a = ORDERS[part][0]
            at = coords_of(part, 0, (me[a] + by) % 4)
            yh, x, z, yl = part_index(at)
            swaps[part, by] = remote(g_ref.at[part, yh, x, z, yl, 1 - core], got.at[part, yh, x, z, yl], partner)
            cp = pltpu.make_async_copy(g_ref.at[part, yh, x, z, yl, core], own.at[part, yh, x, z, yl], lsem.at[k])
            cp.start()
            mine[part, by] = cp
            k += 1

    def add_swap(part, by):
        a = ORDERS[part][0]
        j = (me[a] + by) % 4
        mine[part, by].wait()
        swaps[part, by].wait_recv()

        def body(c):
            i = pick(part, 0, j, c)
            own[i] = own[i] + got[i]
        each(part, 0, body)

    lbuf[0, core] = loss_ref[...]
    lcopy = remote(loss_ref, lbuf.at[0, core], partner)

    for stage in range(3):
        axis = ["x", "y", "z"][stage]
        if stage == 0:
            for part in range(PARTS):
                add_swap(part, 2)
        steps = []
        for part in range(PARTS):
            a = ORDERS[part][stage]
            buf = first[stage * 3 + part]
            src = own.at[(part,) + part_index(coords_of(part, stage, (me[a] + 2) % 4))]
            pre = (full,) * len(block_shape([b for s, b in enumerate(ORDERS[part]) if s > stage]))
            steps.append((
                remote(src.at[pre + (pl.ds(0, 48),)], buf.at[0], sides[a][0]),
                remote(src.at[pre + (pl.ds(48, 48),)], buf.at[1], sides[a][1])))
        if stage == 0:
            lcopy.wait()
            tile = lbuf[0, 0] + lbuf[0, 1]
        else:
            tile = lbuf[stage, 0] + lbuf[stage, 1] + lbuf[stage, 2] + lbuf[stage, 3]
        lbuf[stage + 1, me[axis]] = tile
        mine_l = lbuf.at[stage + 1, me[axis]]
        l_steps = [remote(mine_l, mine_l, sides[axis][0]), remote(mine_l, mine_l, sides[axis][1])]
        if stage == 0:
            for by in (1, 3):
                for part in range(PARTS):
                    add_swap(part, by)
        steps2 = []
        for part in range(PARTS):
            a = ORDERS[part][stage]
            steps[part][0].wait_recv()
            steps[part][1].wait_recv()
            buf = first[stage * 3 + part]

            def body(c):
                r = pick(part, stage, (me[a] + 1) % 4, c)
                l = pick(part, stage, (me[a] + 3) % 4, c)
                p = place(part, stage, c)
                own[r + (pl.ds(0, 48),)] = own[r + (pl.ds(0, 48),)] + buf[(0,) + p]
                own[l + (pl.ds(48, 48),)] = own[l + (pl.ds(48, 48),)] + buf[(1,) + p]
            each(part, stage, body)
            out = second[stage * 3 + part]
            steps2.append((
                remote(own.at[(part,) + part_index(coords_of(part, stage, (me[a] + 1) % 4))], out.at[0], sides[a][0]),
                remote(own.at[(part,) + part_index(coords_of(part, stage, (me[a] + 3) % 4))], out.at[1], sides[a][1])))
        l_steps[0].wait()
        l_steps[1].wait()
        left = (me[axis] + 3) % 4
        far = lbuf.at[stage + 1, left]
        l_far = remote(far, far, sides[axis][0])
        if stage == 0:
            for part in range(PARTS):
                add_swap(part, 0)
        for part in range(PARTS):
            a = ORDERS[part][stage]
            steps2[part][0].wait_recv()
            steps2[part][1].wait_recv()
            out = second[stage * 3 + part]

            def body(c):
                i = pick(part, stage, me[a], c)
                p = place(part, stage, c)
                own[i] = own[i] + out[(0,) + p] + out[(1,) + p]
            each(part, stage, body)
        l_far.wait()
        for pair in steps + steps2:
            pair[0].wait_send()
            pair[1].wait_send()
    for cp in swaps.values():
        cp.wait_send()

    l_out[...] = lbuf[3, 0] + lbuf[3, 1] + lbuf[3, 2] + lbuf[3, 3]
    at = part_index(me)
    for l in range(2):
        for j in range(8):
            k_out[l, :, j * 128:(j + 1) * 128] = own[(l,) + at + (pl.ds(j, 11, stride=8),)]
        for j in range(4):
            q_out[l, :, j * 128:(j + 1) * 128] = own[(2,) + at + (pl.ds(16 * l + j, 4, stride=4),)]
            o_out[l, :, j * 128:(j + 1) * 128] = own[(2,) + at + (pl.ds(32 + 16 * l + j, 4, stride=4),)]
    for r in range(4):
        for j in range(12):
            i = r * 12 + j
            part, row = (0, 88 + i) if i < 8 else (1, 80 + i) if i < 16 else (2, 48 + i)
            h_out[r:r + 1, j * 128:(j + 1) * 128] = own[(part,) + at + (pl.ds(row, 1),)]


def reduce_scatter(g, loss):
    V = pltpu.VMEM
    vm = pl.BlockSpec(memory_space=pltpu.VMEM)
    scratch = [V((PARTS, 2, 4, 4, 2, PROWS, 128), F32), V((PARTS, 2, 4, 4, 2, PROWS, 128), F32), V((4, 4, 8, 128), F32)]
    for rows in (48, PROWS):
        for stage in range(3):
            for part in range(PARTS):
                shape = block_shape(ORDERS[part][stage + 1:])
                scratch.append(V((2,) + shape + (rows, 128), F32))
    n_copies = 12 + 1 + 3 * (12 + 3)
    scratch += [pltpu.SemaphoreType.DMA((n_copies,)), pltpu.SemaphoreType.DMA((n_copies,)), pltpu.SemaphoreType.DMA((12,))]
    return pl.pallas_call(
        reduce_kernel,
        out_shape=(
            jax.ShapeDtypeStruct((2, 11, 2 * DD), F32),
            jax.ShapeDtypeStruct((2, 4, DD), F32),
            jax.ShapeDtypeStruct((2, 4, DD), F32),
            jax.ShapeDtypeStruct((4, PIX), F32),
            jax.ShapeDtypeStruct((8, 128), F32),
        ),
        in_specs=[pl.BlockSpec(memory_space=pl.ANY), vm],
        out_specs=[vm] * 5,
        scratch_shapes=scratch,
        compiler_params=pltpu.CompilerParams(
            collective_id=0, has_side_effects=True, vmem_limit_bytes=60 * 1024 * 1024),
        name="reduce",
    )(g.reshape(PARTS, 2, 4, 4, 2, 2, PROWS, 128), loss)


def shards(features, masked_index, pos_table, mask_token, key_gain, key_weight, query_gain,
           query_weight, out_weight, out_gain, head_weight, target):
    loss, feature_grad, g = compute(
        features, masked_index, pos_table, mask_token, key_gain, key_weight, query_gain,
        query_weight, out_weight, out_gain, head_weight, target)
    key_grad, query_grad, out_grad, head_grad, total = reduce_scatter(g, loss)
    devices = lax.axis_size("tok") * lax.axis_size("clip")
    return total[0, 0] / (devices * ROWS * PIX), feature_grad, key_grad, query_grad, out_grad, head_grad


def solution(mesh):
    both = ("clip", "tok")
    in_specs = (
        P(None, both, None), P(both, None), P(), P(), P(), P(), P(), P(), P(), P(), P(), P(both, None, None))
    out_specs = (
        P(), P(None, both, None), P(None, both, None), P(None, both, None), P(None, both, None), P(both, None))
    return jax.shard_map(shards, mesh=mesh, in_specs=in_specs, out_specs=out_specs, check_vma=False)
```

```python
import math

import jax
import jax.numpy as jnp
from jax import lax
from jax.experimental import pallas as pl
from jax.experimental.pallas import tpu as pltpu
from jax.sharding import PartitionSpec as P

HEADS = 16
HS = 32
VIS = 160
D = 1408
DD = 512
PIX = 1536
ROWS = 1408
TOKS = 1568
CH = 256
EXT = 48
EPS = 1e-6
F32 = jnp.float32
BF = jnp.bfloat16
SCALE = 1.0 / math.sqrt(HS)
LOG2 = SCALE * math.log2(math.e)
GF = 4
GB = 2
SLOT = 3072
NCH = 6


def nn(a, b):
    return lax.dot_general(a, b, (((1,), (0,)), ((), ())), preferred_element_type=F32)


def nt(a, b):
    return lax.dot_general(a, b, (((1,), (1,)), ((), ())), preferred_element_type=F32)


def wide(g, w):
    return jnp.concatenate([g] * (w // 128), axis=1)


def norm(x, gain):
    c = x - jnp.mean(x, axis=0, keepdims=True)
    r = lax.rsqrt(jnp.mean(c * c, axis=0, keepdims=True) + EPS)
    return (c * r * gain).astype(BF), r


def norm_back(dy, n, r, gain):
    n = n.astype(F32)
    m2 = jnp.mean(dy * n, axis=0, keepdims=True)
    dxh = dy * gain
    m1 = jnp.mean(dxh, axis=0, keepdims=True)
    return r * (dxh - m1 - n * (m2 / gain))


def feature_norm(feat_ref, l):
    f = feat_ref[l].astype(F32)
    c = f - jnp.mean(f, axis=1, keepdims=True)
    r = lax.rsqrt(jnp.mean(c * c, axis=1, keepdims=True) + EPS)
    return c * r, r


def attention_back(du, w, tsl, ow, invs, ms, probs, vx, kT, qs, dme, dqs, dkvT):
    dm = nn(ow[...], du).reshape(HEADS, HS, w) * invs[:, tsl].reshape(HEADS, 1, w)
    dm = dm.astype(BF)
    dme[:, 0:HS, 0:w] = dm
    dsum = jnp.sum(dm.astype(F32) * ms[:, tsl].astype(F32).reshape(HEADS, HS, w), axis=1, keepdims=True)
    hi = dsum.astype(BF)
    lo = (dsum - hi.astype(F32)).astype(BF)
    dme[:, HS:EXT, 0:w] = jnp.concatenate([-hi, -lo, jnp.zeros((HEADS, EXT - HS - 2, w), BF)], axis=1)

    def dprobs(h):
        return nn(vx[h], dme[h, :, 0:w])

    def dscores(h, x):
        return (probs(h).astype(F32) * x).astype(BF)

    def rest(h, ds):
        hs = slice(h * HS, (h + 1) * HS)
        vs = slice(DD + h * HS, DD + (h + 1) * HS)
        dqs[hs, tsl] = (nn(kT[hs, :], ds) * SCALE).astype(BF)
        dkvT[hs, :] += nt(qs[hs, tsl], ds)
        dkvT[vs, :] += nt(dme[h, 0:HS, 0:w], probs(h))

    n_g = HEADS // GB
    x = [dprobs(u) for u in range(GB)]
    before = None
    for g in range(n_g):
        x2 = [dprobs((g + 1) * GB + u) for u in range(GB)] if g + 1 < n_g else None
        ds = [dscores(g * GB + u, x[u]) for u in range(GB)]
        if before is not None:
            for u in range(GB):
                rest((g - 1) * GB + u, before[u])
        x, before = x2, ds
    for u in range(GB):
        rest((n_g - 1) * GB + u, before[u])


def make_emit(stage, gsem):
    pending = [[], []]
    count = [0]

    def emit(dot, lhs, rhs, rows, width, share, dsts):
        slot = count[0] % 2
        count[0] += 1
        for cp in pending[slot]:
            cp.wait()
        parts = width // 128
        for c in range(width // 256):
            block = dot(lhs, rhs(c * 256))
            for j in range(2):
                stage[slot, pl.ds(2 * c + j, rows, stride=parts), :] = block[:, j * 128:(j + 1) * 128]
        n = rows * parts
        src = stage.at[slot, pl.ds(0, n)].reshape(n // share, share, 128)
        pending[slot] = []
        for i, (lo, hi, dst) in enumerate(dsts):
            cp = pltpu.make_async_copy(src.at[:, pl.ds(lo, hi - lo)], dst, gsem.at[slot, i])
            cp.start()
            pending[slot].append(cp)

    def finish():
        for cp in pending[0] + pending[1]:
            cp.wait()
        pending[0], pending[1] = [], []

    return emit, finish


def compute_kernel(
    idx_ref, feat_ref, tok_ref, kgain_ref, qgain_ref, ogain_ref,
    pos_hbm, kw_hbm, qw_hbm, ow_hbm, hw_hbm, tgt_hbm,
    loss_ref, g0_hbm, g1_hbm, g2_hbm, nq_hbm, qs_hbm, ms_hbm, dus_hbm, probs_hbm, invs_hbm,
    kT_hbm, vx_hbm, nfT_hbm, d_hbm,
    pos, kw, qw, ow, hw, err, posT, qwT, owT, nf, nfT, k2, vx, vTx, kT, probs0, probs1,
    nq, qs, ms, dus, dqs, no, rs, invs, dkvT, gains, q2, dme, stage, esum, dT, sems, gsem, csem, ksem,
):
    loads = [
        pltpu.make_async_copy(pos_hbm, pos, sems.at[0]),
        pltpu.make_async_copy(kw_hbm, kw, sems.at[1]),
        pltpu.make_async_copy(qw_hbm, qw, sems.at[2]),
        pltpu.make_async_copy(ow_hbm, ow, sems.at[3]),
        pltpu.make_async_copy(hw_hbm, hw, sems.at[4]),
        pltpu.make_async_copy(tgt_hbm.at[0], err, sems.at[5]),
    ]
    for i in (2, 3, 0, 1, 4, 5):
        loads[i].start()

    for i, row in enumerate((qgain_ref[0:1, :], qgain_ref[1:2, :], ogain_ref[...], tok_ref[...])):
        gains[i] = jnp.broadcast_to(row.astype(F32).reshape(1, DD), (128, DD)).T

    for l in range(2):
        n = (feature_norm(feat_ref, l)[0] * kgain_ref[l:l + 1, :].astype(F32)).astype(BF)
        nf[l] = n
        nfT[l] = n.T
    loads[2].wait()
    loads[3].wait()
    for l in range(2):
        qwT[l] = qw[l].T
        owT[l] = ow[l].T
    loads[0].wait()
    posT[...] = pos[...].T
    loads[1].wait()
    tail = jnp.concatenate([jnp.ones((1, VIS), BF), jnp.zeros((EXT - HS - 1, VIS), BF)], axis=0)
    vtail = jnp.concatenate([jnp.ones((VIS, 2), BF), jnp.zeros((VIS, EXT - HS - 2), BF)], axis=1)
    for l in range(2):
        keys = nn(nf[l], kw[l, :, 0:DD]).astype(BF)
        vals = nn(nf[l], kw[l, :, DD:2 * DD]).astype(BF)
        kT[l] = keys.T
        vT = vals.T
        for h in range(HEADS):
            hs = slice(h * HS, (h + 1) * HS)
            k2[l, h] = jnp.concatenate([keys[:, hs], keys[:, hs]], axis=1)
            vx[l, h] = jnp.concatenate([vals[:, hs], vtail], axis=1)
            vTx[l, h] = jnp.concatenate([vT[hs, :], tail], axis=0)
    keep = [
        pltpu.make_async_copy(kT.at[0], kT_hbm, ksem.at[0]),
        pltpu.make_async_copy(vx.at[0], vx_hbm, ksem.at[1]),
        pltpu.make_async_copy(nfT.at[0], nfT_hbm, ksem.at[2]),
    ]
    for cp in keep:
        cp.start()
    dkvT[...] = jnp.zeros_like(dkvT)
    esum[...] = jnp.zeros_like(esum)

    def fwd_layer(l, x, t0, w):
        tsl = pl.ds(t0, w)
        n, r = norm(x, wide(gains[l], w))
        nq[l, :, tsl] = n
        rs[l, :, tsl] = r
        qb = nn(qwT[l], n).astype(BF)
        qs[l, :, tsl] = qb
        qf = qb.astype(F32) * LOG2
        hi = qf.astype(BF)
        lo = (qf - hi.astype(F32)).astype(BF)
        q2[:, 0:HS, 0:w] = hi.reshape(HEADS, HS, w)
        q2[:, HS:2 * HS, 0:w] = lo.reshape(HEADS, HS, w)

        def scores(h):
            return nn(k2[l, h], q2[h, :, 0:w])

        def soft(h, s):
            p = jnp.exp2(s - jnp.max(s, axis=0, keepdims=True)).astype(BF)
            if l == 0:
                probs0[h, :, tsl] = p
            else:
                probs1[h, :, 0:w] = p
            return p

        def mix(h, p):
            o = nn(vTx[l, h], p)
            inv = 1.0 / o[HS:HS + 1]
            invs[l, h:h + 1, tsl] = inv
            ms[l, h * HS:(h + 1) * HS, tsl] = (o[:HS] * inv).astype(BF)

        n_g = HEADS // GF
        s = [scores(u) for u in range(GF)]
        before = None
        for g in range(n_g):
            s2 = [scores((g + 1) * GF + u) for u in range(GF)] if g + 1 < n_g else None
            ps = [soft(g * GF + u, s[u]) for u in range(GF)]
            if before is not None:
                for u in range(GF):
                    mix((g - 1) * GF + u, before[u])
            s, before = s2, ps
        for u in range(GF):
            mix((n_g - 1) * GF + u, before[u])
        return x + nn(owT[l], ms[l, :, tsl])

    def chunk_out(i, t0, w):
        tsl = pl.ds(t0, w)
        pairs = (
            (nq.at[0, :, tsl], nq_hbm.at[:, tsl]), (qs.at[0, :, tsl], qs_hbm.at[:, tsl]),
            (ms.at[0, :, tsl], ms_hbm.at[:, tsl]), (dus.at[0, :, tsl], dus_hbm.at[:, tsl]),
            (probs0.at[:, :, tsl], probs_hbm.at[:, :, tsl]), (invs.at[0, :, tsl], invs_hbm.at[:, tsl]))
        return [pltpu.make_async_copy(a, b, csem.at[k, i]) for k, (a, b) in enumerate(pairs)]

    def chunk_a(i, t0, w):
        tsl = pl.ds(t0, w)
        ids = idx_ref[:, tsl]
        onehot = (lax.broadcasted_iota(jnp.int32, (TOKS, w), 0) == ids).astype(BF)
        x = wide(gains[3], w) + nn(posT[...], onehot)
        x = fwd_layer(0, x, t0, w)
        x = fwd_layer(1, x, t0, w)
        n, r = norm(x, wide(gains[2], w))
        no[:, tsl] = n
        nT = n.T
        e = nn(nT, hw[...]) - err[tsl, :].astype(F32)
        esum[...] += jnp.sum(e * e, axis=0, keepdims=True)
        eb = e.astype(BF)
        err[tsl, :] = eb
        dn = nt(hw[...], eb)
        dx = norm_back(dn, n, r, wide(gains[2], w))
        du = dx.astype(BF)
        dus[1, :, tsl] = du
        attention_back(du, w, tsl, ow.at[1], invs.at[1], ms.at[1], lambda h: probs1[h, :, 0:w], vx.at[1], kT.at[1],
                       qs.at[1], dme, dqs, dkvT)
        dn = nn(qw[1], dqs[:, tsl])
        dx = dx + norm_back(dn, nq[1, :, tsl], rs[1, :, tsl], wide(gains[1], w))
        dus[0, :, tsl] = dx.astype(BF)
        for cp in chunk_out(i, t0, w):
            cp.start()

    loads[4].wait()
    loads[5].wait()
    full = ROWS // CH
    rem = ROWS - full * CH

    @pl.loop(0, full)
    def _(i):
        chunk_a(i, pl.multiple_of(i * CH, CH), CH)

    chunk_a(full, full * CH, rem)

    loss_ref[...] = jnp.full((8, 128), jnp.sum(esum[...]), F32)
    emit, finish = make_emit(stage, gsem)
    for b in range(2):
        to = pl.ds(64 * b, 64)
        emit(nn, no[b * 256:(b + 1) * 256, :], lambda c: err[:, c:c + 256], 256, PIX, 48, [
            (0, 40, g1_hbm.at[to, pl.ds(24, 40)]), (40, 48, g2_hbm.at[to, pl.ds(32, 8)])])
    emit(nt, nq[1], lambda c: dqs[c:c + 256, :], DD, DD, 16, [(0, 16, g2_hbm.at[:, pl.ds(0, 16)])])
    emit(nt, ms[1], lambda c: dus[1, c:c + 256, :], DD, DD, 16, [(0, 16, g2_hbm.at[:, pl.ds(16, 16)])])
    dT[0:DD, :] = (dkvT[0:DD, :] * SCALE).astype(BF)
    dT[DD:2 * DD, :] = dkvT[DD:2 * DD, :].astype(BF)
    keep.append(pltpu.make_async_copy(dT, d_hbm, ksem.at[3]))
    keep[3].start()
    for b in range(4):
        to = pl.ds(32 * b, 32)
        emit(nt, nfT[1, b * 352:(b + 1) * 352, :], lambda c: dT[c:c + 256, :], 352, 2 * DD, 88, [
            (0, 64, g0_hbm.at[to, pl.ds(0, 64)]), (64, 88, g1_hbm.at[to, pl.ds(0, 24)])])
    finish()
    for cp in keep:
        cp.wait()

    @pl.loop(0, full)
    def _(i):
        for cp in chunk_out(i, pl.multiple_of(i * CH, CH), CH):
            cp.wait()

    for cp in chunk_out(full, full * CH, rem):
        cp.wait()


ROWS_1 = (64, 64, 40)
ROWS_2 = (32, 32, 56)


def compute(features, masked_index, pos_table, mask_token, key_gain, key_weight, query_gain,
            query_weight, out_weight, out_gain, head_weight, target):
    vm = pl.BlockSpec(memory_space=pltpu.VMEM)
    hb = pl.BlockSpec(memory_space=pl.ANY)
    S = jax.ShapeDtypeStruct
    out_shape = (
        S((8, 128), F32), *(S((128, r, 128), F32) for r in ROWS_1),
        S((DD, ROWS), BF), S((DD, ROWS), BF), S((DD, ROWS), BF), S((DD, ROWS), BF),
        S((HEADS, VIS, ROWS), BF), S((HEADS, ROWS), F32),
        S((DD, VIS), BF), S((HEADS, VIS, EXT), BF), S((D, VIS), BF), S((2 * DD, VIS), BF),
    )
    V = pltpu.VMEM
    scratch = [
        V((TOKS, DD), BF), V((2, D, 2 * DD), BF), V((2, DD, DD), BF), V((2, DD, DD), BF), V((DD, PIX), BF),
        V((ROWS, PIX), BF), V((DD, TOKS), BF), V((2, DD, DD), BF), V((2, DD, DD), BF),
        V((2, VIS, D), BF), V((2, D, VIS), BF),
        V((2, HEADS, VIS, 2 * HS), BF), V((2, HEADS, VIS, EXT), BF), V((2, HEADS, EXT, VIS), BF), V((2, DD, VIS), BF),
        V((HEADS, VIS, ROWS), BF), V((HEADS, VIS, CH), BF),
        V((2, DD, ROWS), BF), V((2, DD, ROWS), BF), V((2, DD, ROWS), BF), V((2, DD, ROWS), BF), V((DD, ROWS), BF),
        V((DD, ROWS), BF), V((2, 1, ROWS), F32), V((2, HEADS, ROWS), F32), V((2 * DD, VIS), F32),
        V((4, DD, 128), F32), V((HEADS, 2 * HS, CH), BF), V((HEADS, EXT, CH), BF),
        V((2, SLOT, 128), F32), V((1, PIX), F32), V((2 * DD, VIS), BF),
        pltpu.SemaphoreType.DMA((6,)), pltpu.SemaphoreType.DMA((2, 3)), pltpu.SemaphoreType.DMA((6, NCH)),
        pltpu.SemaphoreType.DMA((4,)),
    ]
    return pl.pallas_call(
        compute_kernel,
        out_shape=out_shape,
        in_specs=[vm] * 6 + [hb] * 6,
        out_specs=[vm] + [hb] * 13,
        scratch_shapes=scratch,
        compiler_params=pltpu.CompilerParams(vmem_limit_bytes=63 * 1024 * 1024),
        name="decode",
    )(
        masked_index, features, mask_token, key_gain, query_gain, out_gain,
        pos_table, key_weight, query_weight, out_weight, head_weight, target,
    )


MESH = pl.DeviceIdType.MESH
PARTS = 3
ORDERS = (("x", "y", "z"), ("y", "z", "x"), ("z", "x", "y"))
HALF_1 = (32, 32, 24)
HALF_2 = (16, 16, 32)


def part_index(coords):
    y = coords["y"]
    if isinstance(y, slice):
        return (y, coords["x"], coords["z"], y)
    return (y // 2, coords["x"], coords["z"], y % 2)


def block_shape(free):
    shape = []
    for name, size in (("y", 2), ("x", 4), ("z", 4), ("y", 2)):
        if name in free:
            shape.append(size)
    return tuple(shape)


def reduce_kernel(
    loss_ref, feat_ref, kgain_ref,
    g0, g1, g2, nq_hbm, qs_hbm, ms_hbm, dus_hbm, probs_hbm, invs_hbm, kT_hbm, vx_hbm, nfT_hbm, d_hbm, ow_hbm, kw_hbm,
    k_out, q_out, o_out, h_out, l_out, fgrad_ref,
    nq, qs, ms, dus, probs0, invs, kT, vx, nfT, d1, ow, kw, dqs, dkvT, dT, dme, stage, lbuf,
    send, recv, lsem, csem, ksem, gsem, *rest,
):
    own1, own2, got1, got2 = (rest[3 * i:3 * i + 3] for i in range(4))
    buffers = rest[12:]
    clip, tok = lax.axis_index("clip"), lax.axis_index("tok")
    me = {"x": clip % 4, "y": (clip // 4) * 2 + (tok // 2) % 2, "z": tok // 4}
    core = tok % 2
    full_slice = slice(None)

    def device(c, k):
        return ((c["y"] // 2) * 4 + c["x"], c["z"] * 4 + (c["y"] % 2) * 2 + k)

    def shifted(axis, by):
        c = dict(me)
        c[axis] = (me[axis] + by + 4) % 4
        return c

    partner = device(me, 1 - core)
    sides = {a: (device(shifted(a, 1), core), device(shifted(a, -1), core)) for a in "xyz"}

    chunks = [(i * CH, min(CH, ROWS - i * CH)) for i in range(NCH)]

    def chunk_in(i, t0, w):
        tsl = pl.ds(t0, w)
        pairs = (
            (dus_hbm.at[:, tsl], dus.at[:, tsl]), (invs_hbm.at[:, tsl], invs.at[:, tsl]),
            (ms_hbm.at[:, tsl], ms.at[:, tsl]), (probs_hbm.at[:, :, tsl], probs0.at[:, :, tsl]),
            (qs_hbm.at[:, tsl], qs.at[:, tsl]), (nq_hbm.at[:, tsl], nq.at[:, tsl]))
        return [pltpu.make_async_copy(a, b, csem.at[k, i]) for k, (a, b) in enumerate(pairs)]

    others = [
        pltpu.make_async_copy(ow_hbm.at[0], ow, ksem.at[0]), pltpu.make_async_copy(vx_hbm, vx, ksem.at[1]),
        pltpu.make_async_copy(kT_hbm, kT, ksem.at[2]), pltpu.make_async_copy(nfT_hbm, nfT, ksem.at[3]),
        pltpu.make_async_copy(d_hbm, d1, ksem.at[4]), pltpu.make_async_copy(kw_hbm, kw, ksem.at[5])]
    for cp in others[0:3]:
        cp.start()
    for cp in chunk_in(0, 0, CH):
        cp.start()

    barrier = pltpu.get_barrier_semaphore()
    for dev in [partner] + [d for a in "xyz" for d in sides[a]]:
        pl.semaphore_signal(barrier, inc=1, device_id=dev, device_id_type=MESH)
    pl.semaphore_wait(barrier, 7)

    counter = [0]

    def remote(src, dst, dev):
        i = counter[0]
        counter[0] += 1
        return pltpu.make_async_remote_copy(
            src_ref=src, dst_ref=dst, send_sem=send.at[i], recv_sem=recv.at[i], device_id=dev, device_id_type=MESH)

    class Group:
        def __init__(self, srcs, owns, gots, own_index, bufs, rows, half, base):
            self.srcs, self.owns, self.gots, self.own_index = srcs, owns, gots, own_index
            self.first, self.second, self.rows, self.half = bufs[0:9], bufs[9:18], rows, half
            self.swaps, self.mine = {}, {}
            k = base
            for by in (2, 1, 3, 0):
                for p in range(PARTS):
                    i = part_index(self.coords(p, 0, self.at(p, 0, by)))
                    self.swaps[p, by] = remote(srcs[p].at[i + (1 - core,)], gots[p].at[i], partner)
                    if base is not None:
                        self.mine[p, by] = pltpu.make_async_copy(srcs[p].at[i + (core,)], owns[p].at[i], lsem.at[k])
                        k += 1
            self.step1, self.step2 = {}, {}
            for s in range(3):
                for p in range(PARTS):
                    a = ORDERS[p][s]
                    far = self.block(p, s, 2)
                    pre = (full_slice,) * len(block_shape(ORDERS[p][s + 1:]))
                    lo, hi = pl.ds(0, half[p]), pl.ds(half[p], rows[p] - half[p])
                    f = self.first[s * 3 + p]
                    self.step1[s, p] = (
                        remote(far.at[pre + (lo,)], f.at[(0,) + pre + (lo,)], sides[a][0]),
                        remote(far.at[pre + (hi,)], f.at[(0,) + pre + (hi,)], sides[a][1]))
                    o = self.second[s * 3 + p]
                    self.step2[s, p] = (
                        remote(self.block(p, s, 1), o.at[0], sides[a][0]),
                        remote(self.block(p, s, 3), o.at[1], sides[a][1]))

        def at(self, p, s, by):
            return (me[ORDERS[p][s]] + by) % 4

        def coords(self, p, s, j):
            c = {}
            for t, a in enumerate(ORDERS[p]):
                c[a] = me[a] if t < s else (j if t == s else full_slice)
            return c

        def block(self, p, s, by):
            return self.owns[p].at[part_index(self.coords(p, s, self.at(p, s, by))) + self.own_index]

        def index(self, p, s, by):
            return part_index(self.coords(p, s, self.at(p, s, by)))

        def free(self, p, s):
            return (full_slice,) * len(block_shape(ORDERS[p][s + 1:]))

        def swap(self):
            for by in (2, 1, 3, 0):
                for p in range(PARTS):
                    self.swaps[p, by].start()
                    if self.mine:
                        self.mine[p, by].start()

        def add_swap(self, by):
            for p in range(PARTS):
                if self.mine:
                    self.mine[p, by].wait()
                self.swaps[p, by].wait_recv()

                i = self.index(p, 0, by)
                self.owns[p][i + self.own_index] = self.owns[p][i + self.own_index] + self.gots[p][i]

        def send_far(self, s):
            for p in range(PARTS):
                for cp in self.step1[s, p]:
                    cp.start()

        def send_near(self, s):
            for p in range(PARTS):
                for cp in self.step1[s, p]:
                    cp.wait_recv()
                lo, hi = pl.ds(0, self.half[p]), pl.ds(self.half[p], self.rows[p] - self.half[p])
                own, f = self.owns[p], self.first[s * 3 + p]
                r, l = self.index(p, s, 1) + self.own_index, self.index(p, s, 3) + self.own_index
                i = (0,) + self.free(p, s)
                own[r + (lo,)] = own[r + (lo,)] + f[i + (lo,)]
                own[l + (hi,)] = own[l + (hi,)] + f[i + (hi,)]
                for cp in self.step2[s, p]:
                    cp.start()

        def collect(self, s):
            for p in range(PARTS):
                for cp in self.step2[s, p]:
                    cp.wait_recv()
                own, o = self.owns[p], self.second[s * 3 + p]
                m = self.index(p, s, 0) + self.own_index
                own[m] = own[m] + o[0] + o[1]

        def finish(self):
            for cp in self.swaps.values():
                cp.wait_send()
            for s in range(3):
                for p in range(PARTS):
                    for cp in self.step1[s, p] + self.step2[s, p]:
                        cp.wait_send()

    one = Group((g0, g1, g2), own1, got1, (), buffers[0:18], ROWS_1, HALF_1, 0)
    two = Group(own2, own2, got2, (core,), buffers[18:36], ROWS_2, HALF_2, None)

    one.swap()
    for i, (t0, w) in enumerate(chunks[1:]):
        for cp in chunk_in(i + 1, t0, w):
            cp.start()
    for cp in others[3:]:
        cp.start()
    lbuf[0, core] = loss_ref[...]
    lcopy = remote(loss_ref, lbuf.at[0, core], partner)
    lcopy.start()

    l_near, l_far = [], []
    for s, axis in enumerate("xyz"):
        mine = lbuf.at[s + 1, me[axis]]
        l_near.append([remote(mine, mine, sides[axis][0]), remote(mine, mine, sides[axis][1])])
        far = lbuf.at[s + 1, (me[axis] + 3) % 4]
        l_far.append(remote(far, far, sides[axis][0]))

    def loss_near(s):
        if s == 0:
            lcopy.wait()
            tile = lbuf[0, 0] + lbuf[0, 1]
        else:
            l_far[s - 1].wait()
            tile = lbuf[s, 0] + lbuf[s, 1] + lbuf[s, 2] + lbuf[s, 3]
        lbuf[s + 1, me["xyz"[s]]] = tile
        for cp in l_near[s]:
            cp.start()

    def loss_far(s):
        for cp in l_near[s]:
            cp.wait()
        l_far[s].start()

    dkvT[...] = jnp.zeros_like(dkvT)
    for cp in others[0:3]:
        cp.wait()

    def chunk_b(i, t0, w):
        tsl = pl.ds(t0, w)
        for cp in chunk_in(i, t0, w):
            cp.wait()
        attention_back(dus[:, tsl], w, tsl, ow, invs, ms, lambda h: probs0[h, :, tsl], vx, kT, qs, dme, dqs, dkvT)

    @pl.loop(0, ROWS // CH)
    def _(i):
        chunk_b(i, pl.multiple_of(i * CH, CH), CH)

        @pl.when(i == 1)
        def _():
            one.add_swap(2)
            one.send_far(0)
            loss_near(0)

        @pl.when(i == 4)
        def _():
            one.add_swap(1)
            one.add_swap(3)

    chunk_b(NCH - 1, *chunks[NCH - 1])
    one.send_near(0)
    loss_far(0)

    emit, flush = make_emit(stage, gsem)
    flat = [o.reshape(128, r, 128) for o, r in zip(own2, ROWS_2)]
    emit(nt, nq[...], lambda c: dqs[c:c + 256, :], DD, DD, 16, [(0, 16, flat[2].at[:, pl.ds(24, 16)])])
    emit(nt, ms[...], lambda c: dus[c:c + 256, :], DD, DD, 16, [(0, 16, flat[2].at[:, pl.ds(40, 16)])])
    dT[0:DD, :] = (dkvT[0:DD, :] * SCALE).astype(BF)
    dT[DD:2 * DD, :] = dkvT[DD:2 * DD, :].astype(BF)
    others[3].wait()
    for b in range(4):
        to = pl.ds(32 * b, 32)
        emit(nt, nfT[b * 352:(b + 1) * 352, :], lambda c: dT[c:c + 256, :], 352, 2 * DD, 88, [
            (0, 32, flat[0].at[to]), (32, 64, flat[1].at[to]), (64, 88, flat[2].at[to, pl.ds(0, 24)])])
    flush()
    two.swap()

    def feature_grad(l, d):
        dn = nt(d.T, kw[l])
        xh, r = feature_norm(feat_ref, l)
        dxh = dn * kgain_ref[l:l + 1, :].astype(F32)
        m1 = jnp.mean(dxh, axis=1, keepdims=True)
        m2 = jnp.mean(dxh * xh, axis=1, keepdims=True)
        fgrad_ref[l] = (r * (dxh - m1 - xh * m2)).astype(BF)

    others[4].wait()
    others[5].wait()
    feature_grad(0, dT[...])
    two.add_swap(2)
    two.send_far(0)
    one.add_swap(0)
    feature_grad(1, d1[...])
    one.collect(0)
    one.send_far(1)
    loss_near(1)
    two.add_swap(1)
    two.add_swap(3)
    two.send_near(0)
    one.send_near(1)
    loss_far(1)
    two.add_swap(0)
    one.collect(1)
    one.send_far(2)
    loss_near(2)
    two.collect(0)
    two.send_far(1)
    one.send_near(2)
    loss_far(2)
    two.send_near(1)
    one.collect(2)
    l_far[2].wait()
    l_out[...] = lbuf[3, 0] + lbuf[3, 1] + lbuf[3, 2] + lbuf[3, 3]
    two.collect(1)
    two.send_far(2)
    two.send_near(2)

    at = part_index(me)

    def rows(group, p, start, n, stride=1):
        own = own1 if group == 1 else own2
        ix = at if group == 1 else at + (core,)
        return own[p][ix + ((pl.ds(start, n, stride=stride)),)] if stride > 1 else own[p][ix + (pl.ds(start, n),)]

    for j in range(8):
        k_out[1, 0:8, j * 128:(j + 1) * 128] = rows(1, 0, j, 8, 8)
        k_out[1, 8:11, j * 128:(j + 1) * 128] = rows(1, 1, j, 3, 8)
    for j in range(4):
        q_out[1, :, j * 128:(j + 1) * 128] = rows(1, 2, j, 4, 4)
        o_out[1, :, j * 128:(j + 1) * 128] = rows(1, 2, 16 + j, 4, 4)
    for r in range(4):
        for j in range(12):
            i = r * 12 + j
            h_out[r:r + 1, j * 128:(j + 1) * 128] = rows(1, 1, 24 + i, 1) if i < 40 else rows(1, 2, i - 8, 1)
    two.collect(2)
    for j in range(8):
        lanes = slice(j * 128, (j + 1) * 128)
        k_out[0, 0:4, lanes] = rows(2, 0, j, 4, 8)
        k_out[0, 4:8, lanes] = rows(2, 1, j, 4, 8)
        k_out[0, 8:11, lanes] = rows(2, 2, j, 3, 8)
    for j in range(4):
        lanes = slice(j * 128, (j + 1) * 128)
        q_out[0, :, lanes] = rows(2, 2, 24 + j, 4, 4)
        o_out[0, :, lanes] = rows(2, 2, 40 + j, 4, 4)
    one.finish()
    two.finish()


def reduce_scatter(state, features, key_gain, key_weight, out_weight):
    V = pltpu.VMEM
    vm = pl.BlockSpec(memory_space=pltpu.VMEM)
    hb = pl.BlockSpec(memory_space=pl.ANY)
    S = jax.ShapeDtypeStruct
    loss, parts, rest = state[0], state[1:4], state[4:]
    grid = (2, 4, 4, 2)
    scratch = [
        V((DD, ROWS), BF), V((DD, ROWS), BF), V((DD, ROWS), BF), V((DD, ROWS), BF),
        V((HEADS, VIS, ROWS), BF), V((HEADS, ROWS), F32),
        V((DD, VIS), BF), V((HEADS, VIS, EXT), BF), V((D, VIS), BF), V((2 * DD, VIS), BF),
        V((DD, DD), BF), V((2, D, 2 * DD), BF), V((DD, ROWS), BF), V((2 * DD, VIS), F32), V((2 * DD, VIS), BF),
        V((HEADS, EXT, CH), BF), V((2, SLOT, 128), F32), V((4, 4, 8, 128), F32),
    ]
    n_copies = 2 * (12 + 36) + 1 + 9
    dma = pltpu.SemaphoreType.DMA
    scratch += [dma((n_copies,)), dma((n_copies,)), dma((12,)), dma((6, NCH)), dma((6,)), dma((2, 3))]
    scratch += [V(grid + (r, 128), F32) for r in ROWS_1] + [V(grid + (2, r, 128), F32) for r in ROWS_2]
    scratch += [V(grid + (r, 128), F32) for r in ROWS_1] + [V(grid + (r, 128), F32) for r in ROWS_2]
    for rows in (ROWS_1, ROWS_2):
        for n in (1, 2):
            for s in range(3):
                for p in range(PARTS):
                    scratch.append(V((n,) + block_shape(ORDERS[p][s + 1:]) + (rows[p], 128), F32))
    return pl.pallas_call(
        reduce_kernel,
        out_shape=(
            S((2, 11, 2 * DD), F32), S((2, 4, DD), F32), S((2, 4, DD), F32), S((4, PIX), F32), S((8, 128), F32),
            S((2, VIS, D), BF),
        ),
        in_specs=[vm] * 3 + [hb] * 15,
        out_specs=[vm] * 6,
        scratch_shapes=scratch,
        compiler_params=pltpu.CompilerParams(
            collective_id=0, has_side_effects=True, vmem_limit_bytes=63 * 1024 * 1024),
        name="reduce",
    )(
        loss, features, key_gain, *(g.reshape(grid + (2,) + g.shape[1:]) for g in parts), *rest, out_weight, key_weight)


def output_kernel(loss, k_in, q_in, o_in, h_in, f_in, loss_out, k_out, q_out, o_out, h_out, f_out):
    loss_out[0, 0] = loss[0, 0] * (1.0 / (128 * ROWS * PIX))
    for a, b in ((f_in, f_out), (k_in, k_out), (q_in, q_out), (o_in, o_out), (h_in, h_out)):
        b[...] = a[...]


def outputs(k, q, o, h, loss, f):
    vm = pl.BlockSpec(memory_space=pltpu.VMEM)
    sm = pl.BlockSpec(memory_space=pltpu.SMEM)
    arrays = (k, q, o, h, f)
    return pl.pallas_call(
        output_kernel,
        out_shape=(jax.ShapeDtypeStruct((1, 1), F32), *(jax.ShapeDtypeStruct(a.shape, a.dtype) for a in arrays)),
        in_specs=[sm] + [vm] * 5,
        out_specs=[sm] + [vm] * 5,
        name="outputs",
    )(loss, *arrays)


def shards(features, masked_index, pos_table, mask_token, key_gain, key_weight, query_gain,
           query_weight, out_weight, out_gain, head_weight, target):
    state = compute(
        features, masked_index, pos_table, mask_token, key_gain, key_weight, query_gain,
        query_weight, out_weight, out_gain, head_weight, target)
    summed = reduce_scatter(state, features, key_gain, key_weight, out_weight)
    loss, key_grad, query_grad, out_grad, head_grad, feature_grad = outputs(*summed)
    return loss[0, 0], feature_grad, key_grad, query_grad, out_grad, head_grad


def solution(mesh):
    both = ("clip", "tok")
    in_specs = (
        P(None, both, None), P(both, None), P(), P(), P(), P(), P(), P(), P(), P(), P(), P(both, None, None))
    out_specs = (
        P(), P(None, both, None), P(None, both, None), P(None, both, None), P(None, both, None), P(both, None))
    return jax.shard_map(shards, mesh=mesh, in_specs=in_specs, out_specs=out_specs, check_vma=False)
```

```python
import math

import jax
import jax.numpy as jnp
from jax import lax
from jax.experimental import pallas as pl
from jax.experimental.pallas import tpu as pltpu
from jax.sharding import PartitionSpec as P

HEADS = 16
HS = 32
VIS = 160
D = 1408
DD = 512
PIX = 1536
ROWS = 1408
TOKS = 1568
CH = 256
WIDE = 512
EXT = 48
EPS = 1e-6
F32 = jnp.float32
BF = jnp.bfloat16
SCALE = 1.0 / math.sqrt(HS)
LOG2 = SCALE * math.log2(math.e)
GF = 4
GB = 2
SLOT = 3072
NCH = 6
SPATIAL = 196
MASKED = 176


def nn(a, b):
    return lax.dot_general(a, b, (((1,), (0,)), ((), ())), preferred_element_type=F32)


def nt(a, b):
    return lax.dot_general(a, b, (((1,), (1,)), ((), ())), preferred_element_type=F32)


def wide(g, w):
    return jnp.concatenate([g] * (w // 128), axis=1)


def norm(x, gain):
    c = x - jnp.mean(x, axis=0, keepdims=True)
    r = lax.rsqrt(jnp.mean(c * c, axis=0, keepdims=True) + EPS)
    return (c * r * gain).astype(BF), r


def norm_back(dy, n, r, gain):
    n = n.astype(F32)
    m2 = jnp.mean(dy * n, axis=0, keepdims=True)
    dxh = dy * gain
    m1 = jnp.mean(dxh, axis=0, keepdims=True)
    return r * (dxh - m1 - n * (m2 / gain))


def feature_norm(feat_ref, l):
    f = feat_ref[l].astype(F32)
    c = f - jnp.mean(f, axis=1, keepdims=True)
    r = lax.rsqrt(jnp.mean(c * c, axis=1, keepdims=True) + EPS)
    return c * r, r


def attention_back(du, w, tsl, ow, invs, ms, probs, vx, kT, qs, dme, dqs, dkvT):
    dm = nn(ow[...], du).reshape(HEADS, HS, w) * invs[:, tsl].reshape(HEADS, 1, w)
    dm = dm.astype(BF)
    dme[:, 0:HS, 0:w] = dm
    dsum = jnp.sum(dm.astype(F32) * ms[:, tsl].astype(F32).reshape(HEADS, HS, w), axis=1, keepdims=True)
    hi = dsum.astype(BF)
    lo = (dsum - hi.astype(F32)).astype(BF)
    dme[:, HS:EXT, 0:w] = jnp.concatenate([-hi, -lo, jnp.zeros((HEADS, EXT - HS - 2, w), BF)], axis=1)

    def dprobs(h):
        return nn(vx[h], dme[h, :, 0:w])

    def dscores(h, x):
        return (probs(h).astype(F32) * x).astype(BF)

    def rest(h, ds):
        hs = slice(h * HS, (h + 1) * HS)
        vs = slice(DD + h * HS, DD + (h + 1) * HS)
        dqs[hs, tsl] = (nn(kT[hs, :], ds) * SCALE).astype(BF)
        dkvT[hs, :] += nt(qs[hs, tsl], ds)
        dkvT[vs, :] += nt(dme[h, 0:HS, 0:w], probs(h))

    n_g = HEADS // GB
    x = [dprobs(u) for u in range(GB)]
    before = None
    for g in range(n_g):
        x2 = [dprobs((g + 1) * GB + u) for u in range(GB)] if g + 1 < n_g else None
        ds = [dscores(g * GB + u, x[u]) for u in range(GB)]
        if before is not None:
            for u in range(GB):
                rest((g - 1) * GB + u, before[u])
        x, before = x2, ds
    for u in range(GB):
        rest((n_g - 1) * GB + u, before[u])


def make_emit(stage, gsem):
    pending = [[], []]
    count = [0]

    def emit(dot, lhs, rhs, rows, width, share, dsts):
        slot = count[0] % 2
        count[0] += 1
        for cp in pending[slot]:
            cp.wait()
        parts = width // 128
        for c in range(width // 256):
            block = dot(lhs, rhs(c * 256))
            for j in range(2):
                stage[slot, pl.ds(2 * c + j, rows, stride=parts), :] = block[:, j * 128:(j + 1) * 128]
        n = rows * parts
        src = stage.at[slot, pl.ds(0, n)].reshape(n // share, share, 128)
        pending[slot] = []
        for i, (lo, hi, dst) in enumerate(dsts):
            cp = pltpu.make_async_copy(src.at[:, pl.ds(lo, hi - lo)], dst, gsem.at[slot, i])
            cp.start()
            pending[slot].append(cp)

    def finish():
        for cp in pending[0] + pending[1]:
            cp.wait()
        pending[0], pending[1] = [], []

    return emit, finish


def compute_kernel(
    idx_ref, feat_ref, tok_ref, kgain_ref, qgain_ref, ogain_ref,
    pos_hbm, kw_hbm, qw_hbm, ow_hbm, hw_hbm, tgt_hbm,
    loss_ref, g0_hbm, g1_hbm, g2_hbm, nq_hbm, qs_hbm, ms_hbm, dus_hbm, probs_hbm, invs_hbm,
    kT_hbm, vx_hbm, nfT_hbm, d_hbm,
    pos, kw, qw, ow, hw, err, posT, qwT, owT, nf, nfT, k2, vx, vTx, kT, probs0, probs1,
    nq, qs, ms, dus, dqs, no, rs, invs, dkvT, gains, q2, dme, stage, esum, dT, sems, gsem, csem, ksem,
):
    loads = [
        pltpu.make_async_copy(pos_hbm, pos, sems.at[0]),
        pltpu.make_async_copy(kw_hbm, kw, sems.at[1]),
        pltpu.make_async_copy(qw_hbm, qw, sems.at[2]),
        pltpu.make_async_copy(ow_hbm, ow, sems.at[3]),
        pltpu.make_async_copy(hw_hbm, hw, sems.at[4]),
        pltpu.make_async_copy(tgt_hbm.at[0], err, sems.at[5]),
    ]
    for i in (2, 3, 0, 1, 4, 5):
        loads[i].start()

    for i, row in enumerate((qgain_ref[0:1, :], qgain_ref[1:2, :], ogain_ref[...], tok_ref[...])):
        gains[i] = jnp.broadcast_to(row.astype(F32).reshape(1, DD), (128, DD)).T

    for l in range(2):
        n = (feature_norm(feat_ref, l)[0] * kgain_ref[l:l + 1, :].astype(F32)).astype(BF)
        nf[l] = n
        nfT[l] = n.T
    loads[2].wait()
    loads[3].wait()
    for l in range(2):
        qwT[l] = qw[l].T
        owT[l] = ow[l].T
    loads[0].wait()
    posT[...] = pos[...].T
    loads[1].wait()
    tail = jnp.concatenate([jnp.ones((1, VIS), BF), jnp.zeros((EXT - HS - 1, VIS), BF)], axis=0)
    vtail = jnp.concatenate([jnp.ones((VIS, 2), BF), jnp.zeros((VIS, EXT - HS - 2), BF)], axis=1)
    for l in range(2):
        keys = nn(nf[l], kw[l, :, 0:DD]).astype(BF)
        vals = nn(nf[l], kw[l, :, DD:2 * DD]).astype(BF)
        kT[l] = keys.T
        vT = vals.T
        for h in range(HEADS):
            hs = slice(h * HS, (h + 1) * HS)
            k2[l, h] = jnp.concatenate([keys[:, hs], keys[:, hs]], axis=1)
            vx[l, h] = jnp.concatenate([vals[:, hs], vtail], axis=1)
            vTx[l, h] = jnp.concatenate([vT[hs, :], tail], axis=0)
    keep = [
        pltpu.make_async_copy(kT.at[0], kT_hbm, ksem.at[0]),
        pltpu.make_async_copy(vx.at[0], vx_hbm, ksem.at[1]),
        pltpu.make_async_copy(nfT.at[0], nfT_hbm, ksem.at[2]),
    ]
    for cp in keep:
        cp.start()
    dkvT[...] = jnp.zeros_like(dkvT)
    esum[...] = jnp.zeros_like(esum)

    def fwd_layer(l, x, t0, w):
        tsl = pl.ds(t0, w)
        n, r = norm(x, wide(gains[l], w))
        nq[l, :, tsl] = n
        rs[l, :, tsl] = r
        qb = nn(qwT[l], n).astype(BF)
        qs[l, :, tsl] = qb
        qf = qb.astype(F32) * LOG2
        hi = qf.astype(BF)
        lo = (qf - hi.astype(F32)).astype(BF)
        q2[:, 0:HS, 0:w] = hi.reshape(HEADS, HS, w)
        q2[:, HS:2 * HS, 0:w] = lo.reshape(HEADS, HS, w)

        def scores(h):
            return nn(k2[l, h], q2[h, :, 0:w])

        def soft(h, s):
            p = jnp.exp2(s - jnp.max(s, axis=0, keepdims=True)).astype(BF)
            if l == 0:
                probs0[h, :, tsl] = p
            else:
                probs1[h, :, 0:w] = p
            return p

        def mix(h, p):
            o = nn(vTx[l, h], p)
            inv = 1.0 / o[HS:HS + 1]
            invs[l, h:h + 1, tsl] = inv
            ms[l, h * HS:(h + 1) * HS, tsl] = (o[:HS] * inv).astype(BF)

        n_g = HEADS // GF
        s = [scores(u) for u in range(GF)]
        before = None
        for g in range(n_g):
            s2 = [scores((g + 1) * GF + u) for u in range(GF)] if g + 1 < n_g else None
            ps = [soft(g * GF + u, s[u]) for u in range(GF)]
            if before is not None:
                for u in range(GF):
                    mix((g - 1) * GF + u, before[u])
            s, before = s2, ps
        for u in range(GF):
            mix((n_g - 1) * GF + u, before[u])
        return x + nn(owT[l], ms[l, :, tsl])

    def chunk_out(i, t0, w):
        tsl = pl.ds(t0, w)
        pairs = (
            (nq.at[0, :, tsl], nq_hbm.at[:, tsl]), (qs.at[0, :, tsl], qs_hbm.at[:, tsl]),
            (ms.at[0, :, tsl], ms_hbm.at[:, tsl]), (dus.at[0, :, tsl], dus_hbm.at[:, tsl]),
            (probs0.at[:, :, tsl], probs_hbm.at[:, :, tsl]), (invs.at[0, :, tsl], invs_hbm.at[:, tsl]))
        return [pltpu.make_async_copy(a, b, csem.at[k, i]) for k, (a, b) in enumerate(pairs)]

    def chunk_a(i, t0, w, span):
        tsl = pl.ds(t0, w)
        low = pl.multiple_of(t0 // MASKED * SPATIAL // 128 * 128, 128)
        ids = idx_ref[:, tsl] - low
        onehot = (lax.broadcasted_iota(jnp.int32, (span, w), 0) == ids).astype(BF)
        x = wide(gains[3], w) + nn(posT[:, pl.ds(low, span)], onehot)
        x = fwd_layer(0, x, t0, w)
        x = fwd_layer(1, x, t0, w)
        n, r = norm(x, wide(gains[2], w))
        no[:, tsl] = n
        nT = n.T
        e = nn(nT, hw[...]) - err[tsl, :].astype(F32)
        esum[...] += jnp.sum(e * e, axis=0, keepdims=True)
        eb = e.astype(BF)
        err[tsl, :] = eb
        dn = nt(hw[...], eb)
        dx = norm_back(dn, n, r, wide(gains[2], w))
        du = dx.astype(BF)
        dus[1, :, tsl] = du
        attention_back(du, w, tsl, ow.at[1], invs.at[1], ms.at[1], lambda h: probs1[h, :, 0:w], vx.at[1], kT.at[1],
                       qs.at[1], dme, dqs, dkvT)
        dn = nn(qw[1], dqs[:, tsl])
        dx = dx + norm_back(dn, nq[1, :, tsl], rs[1, :, tsl], wide(gains[1], w))
        dus[0, :, tsl] = dx.astype(BF)
        for cp in chunk_out(i, t0, w):
            cp.start()

    full = ROWS // WIDE
    rem = ROWS - full * WIDE
    frames = 1 + -(-(WIDE - 1) // MASKED)

    @pl.loop(0, full)
    def _(i):
        @pl.when(i == 0)
        def _():
            loads[4].wait()
            loads[5].wait()

        chunk_a(i, pl.multiple_of(i * WIDE, WIDE), WIDE, -(-(frames * SPATIAL + 127) // 128) * 128)

    chunk_a(full, full * WIDE, rem, TOKS - full * WIDE // MASKED * SPATIAL // 128 * 128)

    loss_ref[...] = jnp.full((8, 128), jnp.sum(esum[...]), F32)
    emit, finish = make_emit(stage, gsem)
    for b in range(2):
        to = pl.ds(64 * b, 64)
        emit(nn, no[b * 256:(b + 1) * 256, :], lambda c: err[:, c:c + 256], 256, PIX, 48, [
            (0, 40, g1_hbm.at[to, pl.ds(24, 40)]), (40, 48, g2_hbm.at[to, pl.ds(32, 8)])])
    emit(nt, nq[1], lambda c: dqs[c:c + 256, :], DD, DD, 16, [(0, 16, g2_hbm.at[:, pl.ds(0, 16)])])
    emit(nt, ms[1], lambda c: dus[1, c:c + 256, :], DD, DD, 16, [(0, 16, g2_hbm.at[:, pl.ds(16, 16)])])
    dT[0:DD, :] = (dkvT[0:DD, :] * SCALE).astype(BF)
    dT[DD:2 * DD, :] = dkvT[DD:2 * DD, :].astype(BF)
    keep.append(pltpu.make_async_copy(dT, d_hbm, ksem.at[3]))
    keep[3].start()
    for b in range(4):
        to = pl.ds(32 * b, 32)
        emit(nt, nfT[1, b * 352:(b + 1) * 352, :], lambda c: dT[c:c + 256, :], 352, 2 * DD, 88, [
            (0, 64, g0_hbm.at[to, pl.ds(0, 64)]), (64, 88, g1_hbm.at[to, pl.ds(0, 24)])])
    finish()
    for cp in keep:
        cp.wait()

    for i in range(full + 1):
        for cp in chunk_out(i, i * WIDE, min(WIDE, ROWS - i * WIDE)):
            cp.wait()


ROWS_1 = (64, 64, 40)
ROWS_2 = (32, 32, 56)


def compute(features, masked_index, pos_table, mask_token, key_gain, key_weight, query_gain,
            query_weight, out_weight, out_gain, head_weight, target):
    vm = pl.BlockSpec(memory_space=pltpu.VMEM)
    hb = pl.BlockSpec(memory_space=pl.ANY)
    S = jax.ShapeDtypeStruct
    out_shape = (
        S((8, 128), F32), *(S((128, r, 128), F32) for r in ROWS_1),
        S((DD, ROWS), BF), S((DD, ROWS), BF), S((DD, ROWS), BF), S((DD, ROWS), BF),
        S((HEADS, VIS, ROWS), BF), S((HEADS, ROWS), F32),
        S((DD, VIS), BF), S((HEADS, VIS, EXT), BF), S((D, VIS), BF), S((2 * DD, VIS), BF),
    )
    V = pltpu.VMEM
    scratch = [
        V((TOKS, DD), BF), V((2, D, 2 * DD), BF), V((2, DD, DD), BF), V((2, DD, DD), BF), V((DD, PIX), BF),
        V((ROWS, PIX), BF), V((DD, TOKS), BF), V((2, DD, DD), BF), V((2, DD, DD), BF),
        V((2, VIS, D), BF), V((2, D, VIS), BF),
        V((2, HEADS, VIS, 2 * HS), BF), V((2, HEADS, VIS, EXT), BF), V((2, HEADS, EXT, VIS), BF), V((2, DD, VIS), BF),
        V((HEADS, VIS, ROWS), BF), V((HEADS, VIS, WIDE), BF),
        V((2, DD, ROWS), BF), V((2, DD, ROWS), BF), V((2, DD, ROWS), BF), V((2, DD, ROWS), BF), V((DD, ROWS), BF),
        V((DD, ROWS), BF), V((2, 1, ROWS), F32), V((2, HEADS, ROWS), F32), V((2 * DD, VIS), F32),
        V((4, DD, 128), F32), V((HEADS, 2 * HS, WIDE), BF), V((HEADS, EXT, WIDE), BF),
        V((2, SLOT, 128), F32), V((1, PIX), F32), V((2 * DD, VIS), BF),
        pltpu.SemaphoreType.DMA((6,)), pltpu.SemaphoreType.DMA((2, 3)), pltpu.SemaphoreType.DMA((6, NCH)),
        pltpu.SemaphoreType.DMA((4,)),
    ]
    return pl.pallas_call(
        compute_kernel,
        out_shape=out_shape,
        in_specs=[vm] * 6 + [hb] * 6,
        out_specs=[vm] + [hb] * 13,
        scratch_shapes=scratch,
        compiler_params=pltpu.CompilerParams(vmem_limit_bytes=63 * 1024 * 1024),
        name="decode",
    )(
        masked_index, features, mask_token, key_gain, query_gain, out_gain,
        pos_table, key_weight, query_weight, out_weight, head_weight, target,
    )


MESH = pl.DeviceIdType.MESH
PARTS = 3
ORDERS = (("x", "y", "z"), ("y", "z", "x"), ("z", "x", "y"))
HALF_1 = (32, 32, 24)
HALF_2 = (16, 16, 32)


def part_index(coords):
    y = coords["y"]
    if isinstance(y, slice):
        return (y, coords["x"], coords["z"], y)
    return (y // 2, coords["x"], coords["z"], y % 2)


def block_shape(free):
    shape = []
    for name, size in (("y", 2), ("x", 4), ("z", 4), ("y", 2)):
        if name in free:
            shape.append(size)
    return tuple(shape)


def reduce_kernel(
    loss_ref, feat_ref, kgain_ref,
    g0, g1, g2, nq_hbm, qs_hbm, ms_hbm, dus_hbm, probs_hbm, invs_hbm, kT_hbm, vx_hbm, nfT_hbm, d_hbm, ow_hbm, kw_hbm,
    k_out, q_out, o_out, h_out, l_out, fgrad_ref,
    nq, qs, ms, dus, probs0, invs, kT, vx, nfT, d1, ow, kw, dqs, dkvT, dT, dme, stage, lbuf,
    send, recv, lsem, csem, ksem, gsem, *rest,
):
    own1, own2, got1, got2 = (rest[3 * i:3 * i + 3] for i in range(4))
    buffers = rest[12:]
    clip, tok = lax.axis_index("clip"), lax.axis_index("tok")
    me = {"x": clip % 4, "y": (clip // 4) * 2 + (tok // 2) % 2, "z": tok // 4}
    core = tok % 2
    full_slice = slice(None)

    def device(c, k):
        return ((c["y"] // 2) * 4 + c["x"], c["z"] * 4 + (c["y"] % 2) * 2 + k)

    def shifted(axis, by):
        c = dict(me)
        c[axis] = (me[axis] + by + 4) % 4
        return c

    partner = device(me, 1 - core)
    sides = {a: (device(shifted(a, 1), core), device(shifted(a, -1), core)) for a in "xyz"}

    chunks = [(i * CH, min(CH, ROWS - i * CH)) for i in range(NCH)]

    def chunk_in(i, t0, w):
        tsl = pl.ds(t0, w)
        pairs = (
            (dus_hbm.at[:, tsl], dus.at[:, tsl]), (invs_hbm.at[:, tsl], invs.at[:, tsl]),
            (ms_hbm.at[:, tsl], ms.at[:, tsl]), (probs_hbm.at[:, :, tsl], probs0.at[:, :, tsl]),
            (qs_hbm.at[:, tsl], qs.at[:, tsl]), (nq_hbm.at[:, tsl], nq.at[:, tsl]))
        return [pltpu.make_async_copy(a, b, csem.at[k, i]) for k, (a, b) in enumerate(pairs)]

    others = [
        pltpu.make_async_copy(ow_hbm.at[0], ow, ksem.at[0]), pltpu.make_async_copy(vx_hbm, vx, ksem.at[1]),
        pltpu.make_async_copy(kT_hbm, kT, ksem.at[2]), pltpu.make_async_copy(nfT_hbm, nfT, ksem.at[3]),
        pltpu.make_async_copy(d_hbm, d1, ksem.at[4]), pltpu.make_async_copy(kw_hbm, kw, ksem.at[5])]
    for cp in others[0:3]:
        cp.start()
    for cp in chunk_in(0, 0, CH):
        cp.start()

    barrier = pltpu.get_barrier_semaphore()
    for dev in [partner] + [d for a in "xyz" for d in sides[a]]:
        pl.semaphore_signal(barrier, inc=1, device_id=dev, device_id_type=MESH)
    pl.semaphore_wait(barrier, 7)

    counter = [0]

    def remote(src, dst, dev):
        i = counter[0]
        counter[0] += 1
        return pltpu.make_async_remote_copy(
            src_ref=src, dst_ref=dst, send_sem=send.at[i], recv_sem=recv.at[i], device_id=dev, device_id_type=MESH)

    class Group:
        def __init__(self, srcs, owns, gots, own_index, bufs, rows, half, base):
            self.srcs, self.owns, self.gots, self.own_index = srcs, owns, gots, own_index
            self.first, self.second, self.rows, self.half = bufs[0:9], bufs[9:18], rows, half
            self.swaps, self.mine = {}, {}
            k = base
            for by in (2, 1, 3, 0):
                for p in range(PARTS):
                    i = part_index(self.coords(p, 0, self.at(p, 0, by)))
                    self.swaps[p, by] = remote(srcs[p].at[i + (1 - core,)], gots[p].at[i], partner)
                    if base is not None:
                        self.mine[p, by] = pltpu.make_async_copy(srcs[p].at[i + (core,)], owns[p].at[i], lsem.at[k])
                        k += 1
            self.step1, self.step2 = {}, {}
            for s in range(3):
                for p in range(PARTS):
                    a = ORDERS[p][s]
                    far = self.block(p, s, 2)
                    pre = (full_slice,) * len(block_shape(ORDERS[p][s + 1:]))
                    lo, hi = pl.ds(0, half[p]), pl.ds(half[p], rows[p] - half[p])
                    f = self.first[s * 3 + p]
                    self.step1[s, p] = (
                        remote(far.at[pre + (lo,)], f.at[(0,) + pre + (lo,)], sides[a][0]),
                        remote(far.at[pre + (hi,)], f.at[(0,) + pre + (hi,)], sides[a][1]))
                    o = self.second[s * 3 + p]
                    self.step2[s, p] = (
                        remote(self.block(p, s, 1), o.at[0], sides[a][0]),
                        remote(self.block(p, s, 3), o.at[1], sides[a][1]))

        def at(self, p, s, by):
            return (me[ORDERS[p][s]] + by) % 4

        def coords(self, p, s, j):
            c = {}
            for t, a in enumerate(ORDERS[p]):
                c[a] = me[a] if t < s else (j if t == s else full_slice)
            return c

        def block(self, p, s, by):
            return self.owns[p].at[part_index(self.coords(p, s, self.at(p, s, by))) + self.own_index]

        def index(self, p, s, by):
            return part_index(self.coords(p, s, self.at(p, s, by)))

        def free(self, p, s):
            return (full_slice,) * len(block_shape(ORDERS[p][s + 1:]))

        def swap(self):
            for by in (2, 1, 3, 0):
                for p in range(PARTS):
                    self.swaps[p, by].start()
                    if self.mine:
                        self.mine[p, by].start()

        def add_swap(self, by):
            for p in range(PARTS):
                if self.mine:
                    self.mine[p, by].wait()
                self.swaps[p, by].wait_recv()

                i = self.index(p, 0, by)
                self.owns[p][i + self.own_index] = self.owns[p][i + self.own_index] + self.gots[p][i]

        def send_far(self, s):
            for p in range(PARTS):
                for cp in self.step1[s, p]:
                    cp.start()

        def send_near(self, s):
            for p in range(PARTS):
                for cp in self.step1[s, p]:
                    cp.wait_recv()
                lo, hi = pl.ds(0, self.half[p]), pl.ds(self.half[p], self.rows[p] - self.half[p])
                own, f = self.owns[p], self.first[s * 3 + p]
                r, l = self.index(p, s, 1) + self.own_index, self.index(p, s, 3) + self.own_index
                i = (0,) + self.free(p, s)
                own[r + (lo,)] = own[r + (lo,)] + f[i + (lo,)]
                own[l + (hi,)] = own[l + (hi,)] + f[i + (hi,)]
                for cp in self.step2[s, p]:
                    cp.start()

        def collect(self, s):
            for p in range(PARTS):
                for cp in self.step2[s, p]:
                    cp.wait_recv()
                own, o = self.owns[p], self.second[s * 3 + p]
                m = self.index(p, s, 0) + self.own_index
                own[m] = own[m] + o[0] + o[1]

        def finish(self):
            for cp in self.swaps.values():
                cp.wait_send()
            for s in range(3):
                for p in range(PARTS):
                    for cp in self.step1[s, p] + self.step2[s, p]:
                        cp.wait_send()

    one = Group((g0, g1, g2), own1, got1, (), buffers[0:18], ROWS_1, HALF_1, 0)
    two = Group(own2, own2, got2, (core,), buffers[18:36], ROWS_2, HALF_2, None)

    one.swap()
    for i, (t0, w) in enumerate(chunks[1:]):
        for cp in chunk_in(i + 1, t0, w):
            cp.start()
    for cp in others[3:]:
        cp.start()
    lbuf[0, core] = loss_ref[...]
    lcopy = remote(loss_ref, lbuf.at[0, core], partner)
    lcopy.start()

    l_near, l_far = [], []
    for s, axis in enumerate("xyz"):
        mine = lbuf.at[s + 1, me[axis]]
        l_near.append([remote(mine, mine, sides[axis][0]), remote(mine, mine, sides[axis][1])])
        far = lbuf.at[s + 1, (me[axis] + 3) % 4]
        l_far.append(remote(far, far, sides[axis][0]))

    def loss_near(s):
        if s == 0:
            lcopy.wait()
            tile = lbuf[0, 0] + lbuf[0, 1]
        else:
            l_far[s - 1].wait()
            tile = lbuf[s, 0] + lbuf[s, 1] + lbuf[s, 2] + lbuf[s, 3]
        lbuf[s + 1, me["xyz"[s]]] = tile
        for cp in l_near[s]:
            cp.start()

    def loss_far(s):
        for cp in l_near[s]:
            cp.wait()
        l_far[s].start()

    dkvT[...] = jnp.zeros_like(dkvT)
    for cp in others[0:3]:
        cp.wait()

    def chunk_b(i, t0, w):
        tsl = pl.ds(t0, w)
        for cp in chunk_in(i, t0, w):
            cp.wait()
        attention_back(dus[:, tsl], w, tsl, ow, invs, ms, lambda h: probs0[h, :, tsl], vx, kT, qs, dme, dqs, dkvT)

    @pl.loop(0, ROWS // CH)
    def _(i):
        chunk_b(i, pl.multiple_of(i * CH, CH), CH)

        @pl.when(i == 1)
        def _():
            one.add_swap(2)
            one.send_far(0)
            loss_near(0)

        @pl.when(i == 4)
        def _():
            one.add_swap(1)
            one.add_swap(3)

    chunk_b(NCH - 1, *chunks[NCH - 1])
    one.send_near(0)
    loss_far(0)

    emit, flush = make_emit(stage, gsem)
    flat = [o.reshape(128, r, 128) for o, r in zip(own2, ROWS_2)]
    emit(nt, nq[...], lambda c: dqs[c:c + 256, :], DD, DD, 16, [(0, 16, flat[2].at[:, pl.ds(24, 16)])])
    emit(nt, ms[...], lambda c: dus[c:c + 256, :], DD, DD, 16, [(0, 16, flat[2].at[:, pl.ds(40, 16)])])
    dT[0:DD, :] = (dkvT[0:DD, :] * SCALE).astype(BF)
    dT[DD:2 * DD, :] = dkvT[DD:2 * DD, :].astype(BF)
    others[3].wait()
    for b in range(4):
        to = pl.ds(32 * b, 32)
        emit(nt, nfT[b * 352:(b + 1) * 352, :], lambda c: dT[c:c + 256, :], 352, 2 * DD, 88, [
            (0, 32, flat[0].at[to]), (32, 64, flat[1].at[to]), (64, 88, flat[2].at[to, pl.ds(0, 24)])])
    flush()
    two.swap()

    def feature_grad(l, d):
        dn = nt(d.T, kw[l])
        xh, r = feature_norm(feat_ref, l)
        dxh = dn * kgain_ref[l:l + 1, :].astype(F32)
        m1 = jnp.mean(dxh, axis=1, keepdims=True)
        m2 = jnp.mean(dxh * xh, axis=1, keepdims=True)
        fgrad_ref[l] = (r * (dxh - m1 - xh * m2)).astype(BF)

    others[4].wait()
    others[5].wait()
    feature_grad(0, dT[...])
    two.add_swap(2)
    two.send_far(0)
    one.add_swap(0)
    feature_grad(1, d1[...])
    one.collect(0)
    one.send_far(1)
    loss_near(1)
    two.add_swap(1)
    two.add_swap(3)
    two.send_near(0)
    one.send_near(1)
    loss_far(1)
    two.add_swap(0)
    one.collect(1)
    one.send_far(2)
    loss_near(2)
    two.collect(0)
    two.send_far(1)
    one.send_near(2)
    loss_far(2)
    two.send_near(1)
    one.collect(2)
    l_far[2].wait()
    l_out[...] = lbuf[3, 0] + lbuf[3, 1] + lbuf[3, 2] + lbuf[3, 3]
    two.collect(1)
    two.send_far(2)
    two.send_near(2)

    at = part_index(me)

    def rows(group, p, start, n, stride=1):
        own = own1 if group == 1 else own2
        ix = at if group == 1 else at + (core,)
        return own[p][ix + ((pl.ds(start, n, stride=stride)),)] if stride > 1 else own[p][ix + (pl.ds(start, n),)]

    for j in range(8):
        k_out[1, 0:8, j * 128:(j + 1) * 128] = rows(1, 0, j, 8, 8)
        k_out[1, 8:11, j * 128:(j + 1) * 128] = rows(1, 1, j, 3, 8)
    for j in range(4):
        q_out[1, :, j * 128:(j + 1) * 128] = rows(1, 2, j, 4, 4)
        o_out[1, :, j * 128:(j + 1) * 128] = rows(1, 2, 16 + j, 4, 4)
    for r in range(4):
        for j in range(12):
            i = r * 12 + j
            h_out[r:r + 1, j * 128:(j + 1) * 128] = rows(1, 1, 24 + i, 1) if i < 40 else rows(1, 2, i - 8, 1)
    two.collect(2)
    for j in range(8):
        lanes = slice(j * 128, (j + 1) * 128)
        k_out[0, 0:4, lanes] = rows(2, 0, j, 4, 8)
        k_out[0, 4:8, lanes] = rows(2, 1, j, 4, 8)
        k_out[0, 8:11, lanes] = rows(2, 2, j, 3, 8)
    for j in range(4):
        lanes = slice(j * 128, (j + 1) * 128)
        q_out[0, :, lanes] = rows(2, 2, 24 + j, 4, 4)
        o_out[0, :, lanes] = rows(2, 2, 40 + j, 4, 4)
    one.finish()
    two.finish()


def reduce_scatter(state, features, key_gain, key_weight, out_weight):
    V = pltpu.VMEM
    vm = pl.BlockSpec(memory_space=pltpu.VMEM)
    hb = pl.BlockSpec(memory_space=pl.ANY)
    S = jax.ShapeDtypeStruct
    loss, parts, rest = state[0], state[1:4], state[4:]
    grid = (2, 4, 4, 2)
    scratch = [
        V((DD, ROWS), BF), V((DD, ROWS), BF), V((DD, ROWS), BF), V((DD, ROWS), BF),
        V((HEADS, VIS, ROWS), BF), V((HEADS, ROWS), F32),
        V((DD, VIS), BF), V((HEADS, VIS, EXT), BF), V((D, VIS), BF), V((2 * DD, VIS), BF),
        V((DD, DD), BF), V((2, D, 2 * DD), BF), V((DD, ROWS), BF), V((2 * DD, VIS), F32), V((2 * DD, VIS), BF),
        V((HEADS, EXT, CH), BF), V((2, SLOT, 128), F32), V((4, 4, 8, 128), F32),
    ]
    n_copies = 2 * (12 + 36) + 1 + 9
    dma = pltpu.SemaphoreType.DMA
    scratch += [dma((n_copies,)), dma((n_copies,)), dma((12,)), dma((6, NCH)), dma((6,)), dma((2, 3))]
    scratch += [V(grid + (r, 128), F32) for r in ROWS_1] + [V(grid + (2, r, 128), F32) for r in ROWS_2]
    scratch += [V(grid + (r, 128), F32) for r in ROWS_1] + [V(grid + (r, 128), F32) for r in ROWS_2]
    for rows in (ROWS_1, ROWS_2):
        for n in (1, 2):
            for s in range(3):
                for p in range(PARTS):
                    scratch.append(V((n,) + block_shape(ORDERS[p][s + 1:]) + (rows[p], 128), F32))
    return pl.pallas_call(
        reduce_kernel,
        out_shape=(
            S((2, 11, 2 * DD), F32), S((2, 4, DD), F32), S((2, 4, DD), F32), S((4, PIX), F32), S((8, 128), F32),
            S((2, VIS, D), BF),
        ),
        in_specs=[vm] * 3 + [hb] * 15,
        out_specs=[vm] * 6,
        scratch_shapes=scratch,
        compiler_params=pltpu.CompilerParams(
            collective_id=0, has_side_effects=True, vmem_limit_bytes=63 * 1024 * 1024),
        name="reduce",
    )(
        loss, features, key_gain, *(g.reshape(grid + (2,) + g.shape[1:]) for g in parts), *rest, out_weight, key_weight)


def output_kernel(loss, k_in, q_in, o_in, h_in, f_in, loss_out, k_out, q_out, o_out, h_out, f_out):
    loss_out[0, 0] = loss[0, 0] * (1.0 / (128 * ROWS * PIX))
    for l in range(2):
        k_out[:, l, :] = k_in[l]
    for a, b in ((f_in, f_out), (q_in, q_out), (o_in, o_out), (h_in, h_out)):
        b[...] = a[...]


def outputs(k, q, o, h, loss, f):
    vm = pl.BlockSpec(memory_space=pltpu.VMEM)
    sm = pl.BlockSpec(memory_space=pltpu.SMEM)
    arrays = (k, q, o, h, f)
    return pl.pallas_call(
        output_kernel,
        out_shape=(jax.ShapeDtypeStruct((1, 1), F32), jax.ShapeDtypeStruct((11, 2, 2 * DD), F32),
                   *(jax.ShapeDtypeStruct(a.shape, a.dtype) for a in arrays[1:])),
        in_specs=[sm] + [vm] * 5,
        out_specs=[sm] + [vm] * 5,
        name="outputs",
    )(loss, *arrays)


def shards(features, masked_index, pos_table, mask_token, key_gain, key_weight, query_gain,
           query_weight, out_weight, out_gain, head_weight, target):
    state = compute(
        features, masked_index, pos_table, mask_token, key_gain, key_weight, query_gain,
        query_weight, out_weight, out_gain, head_weight, target)
    summed = reduce_scatter(state, features, key_gain, key_weight, out_weight)
    loss, key_grad, query_grad, out_grad, head_grad, feature_grad = outputs(*summed)
    return loss[0, 0], feature_grad, key_grad.transpose(1, 0, 2), query_grad, out_grad, head_grad


def solution(mesh):
    both = ("clip", "tok")
    in_specs = (
        P(None, both, None), P(both, None), P(), P(), P(), P(), P(), P(), P(), P(), P(), P(both, None, None))
    out_specs = (
        P(), P(None, both, None), P(None, both, None), P(None, both, None), P(None, both, None), P(both, None))
    return jax.shard_map(shards, mesh=mesh, in_specs=in_specs, out_specs=out_specs, check_vma=False)
```

```python
import math

import jax
import jax.numpy as jnp
from jax import lax
from jax.experimental import pallas as pl
from jax.experimental.pallas import tpu as pltpu
from jax.sharding import PartitionSpec as P

HEADS = 16
HS = 32
VIS = 160
D = 1408
DD = 512
PIX = 1536
ROWS = 1408
TOKS = 1568
CH = 256
WIDE = 512
EXT = 48
EPS = 1e-6
F32 = jnp.float32
BF = jnp.bfloat16
SCALE = 1.0 / math.sqrt(HS)
LOG2 = SCALE * math.log2(math.e)
GF = 4
GB = 2
SLOT = 3072
NCH = 6
SPATIAL = 196
MASKED = 176


def nn(a, b):
    return lax.dot_general(a, b, (((1,), (0,)), ((), ())), preferred_element_type=F32)


def nt(a, b):
    return lax.dot_general(a, b, (((1,), (1,)), ((), ())), preferred_element_type=F32)


def wide(g, w):
    return jnp.concatenate([g] * (w // 128), axis=1)


def norm(x, gain):
    c = x - jnp.mean(x, axis=0, keepdims=True)
    r = lax.rsqrt(jnp.mean(c * c, axis=0, keepdims=True) + EPS)
    return (c * r * gain).astype(BF), r


def norm_back(dy, n, r, gain):
    n = n.astype(F32)
    m2 = jnp.mean(dy * n, axis=0, keepdims=True)
    dxh = dy * gain
    m1 = jnp.mean(dxh, axis=0, keepdims=True)
    return r * (dxh - m1 - n * (m2 / gain))


def feature_norm(feat_ref, l):
    f = feat_ref[l].astype(F32)
    c = f - jnp.mean(f, axis=1, keepdims=True)
    r = lax.rsqrt(jnp.mean(c * c, axis=1, keepdims=True) + EPS)
    return c * r, r


def attention_back(du, w, tsl, ow, invs, ms, probs, vx, kT, qs, dme, dqs, dkvT):
    dm = nn(ow[...], du).reshape(HEADS, HS, w) * invs[:, tsl].reshape(HEADS, 1, w)
    dm = dm.astype(BF)
    dme[:, 0:HS, 0:w] = dm
    dsum = jnp.sum(dm.astype(F32) * ms[:, tsl].astype(F32).reshape(HEADS, HS, w), axis=1, keepdims=True)
    hi = dsum.astype(BF)
    lo = (dsum - hi.astype(F32)).astype(BF)
    dme[:, HS:EXT, 0:w] = jnp.concatenate([-hi, -lo, jnp.zeros((HEADS, EXT - HS - 2, w), BF)], axis=1)

    def dprobs(h):
        return nn(vx[h], dme[h, :, 0:w])

    def dscores(h, x):
        return (probs(h).astype(F32) * x).astype(BF)

    def rest(h, ds):
        hs = slice(h * HS, (h + 1) * HS)
        vs = slice(DD + h * HS, DD + (h + 1) * HS)
        dqs[hs, tsl] = (nn(kT[hs, :], ds) * SCALE).astype(BF)
        dkvT[hs, :] += nt(qs[hs, tsl], ds)
        dkvT[vs, :] += nt(dme[h, 0:HS, 0:w], probs(h))

    n_g = HEADS // GB
    x = [dprobs(u) for u in range(GB)]
    before = None
    for g in range(n_g):
        x2 = [dprobs((g + 1) * GB + u) for u in range(GB)] if g + 1 < n_g else None
        ds = [dscores(g * GB + u, x[u]) for u in range(GB)]
        if before is not None:
            for u in range(GB):
                rest((g - 1) * GB + u, before[u])
        x, before = x2, ds
    for u in range(GB):
        rest((n_g - 1) * GB + u, before[u])


def make_emit(stage, gsem):
    pending = [[], []]
    count = [0]

    def emit(dot, lhs, rhs, rows, width, share, dsts):
        slot = count[0] % 2
        count[0] += 1
        for cp in pending[slot]:
            cp.wait()
        parts = width // 128
        for c in range(width // 256):
            block = dot(lhs, rhs(c * 256))
            for j in range(2):
                stage[slot, pl.ds(2 * c + j, rows, stride=parts), :] = block[:, j * 128:(j + 1) * 128]
        n = rows * parts
        src = stage.at[slot, pl.ds(0, n)].reshape(n // share, share, 128)
        pending[slot] = []
        for i, (lo, hi, dst) in enumerate(dsts):
            cp = pltpu.make_async_copy(src.at[:, pl.ds(lo, hi - lo)], dst, gsem.at[slot, i])
            cp.start()
            pending[slot].append(cp)

    def finish():
        for cp in pending[0] + pending[1]:
            cp.wait()
        pending[0], pending[1] = [], []

    return emit, finish


def compute_kernel(
    idx_ref, feat_ref, tok_ref, kgain_ref, qgain_ref, ogain_ref,
    pos_hbm, kw_hbm, qw_hbm, ow_hbm, hw_hbm, tgt_hbm,
    loss_ref, g0_hbm, g1_hbm, g2_hbm, nq_hbm, qs_hbm, ms_hbm, dus_hbm, probs_hbm, invs_hbm,
    kT_hbm, vx_hbm, nfT_hbm, d_hbm,
    pos, kw, qw, ow, hw, err, posT, qwT, owT, nf, nfT, k2, vx, vTx, kT, probs0, probs1,
    nq, qs, ms, dus, dqs, no, rs, invs, dkvT, gains, q2, dme, stage, esum, dT, sems, gsem, csem, ksem,
):
    loads = [
        pltpu.make_async_copy(pos_hbm, pos, sems.at[0]),
        pltpu.make_async_copy(kw_hbm, kw, sems.at[1]),
        pltpu.make_async_copy(qw_hbm, qw, sems.at[2]),
        pltpu.make_async_copy(ow_hbm, ow, sems.at[3]),
        pltpu.make_async_copy(hw_hbm, hw, sems.at[4]),
        pltpu.make_async_copy(tgt_hbm.at[0], err, sems.at[5]),
    ]
    for i in (2, 3, 0, 1, 4, 5):
        loads[i].start()

    for i, row in enumerate((qgain_ref[0:1, :], qgain_ref[1:2, :], ogain_ref[...], tok_ref[...])):
        gains[i] = jnp.broadcast_to(row.astype(F32).reshape(1, DD), (128, DD)).T

    for l in range(2):
        n = (feature_norm(feat_ref, l)[0] * kgain_ref[l:l + 1, :].astype(F32)).astype(BF)
        nf[l] = n
        nfT[l] = n.T
    loads[2].wait()
    loads[3].wait()
    for l in range(2):
        qwT[l] = qw[l].T
        owT[l] = ow[l].T
    loads[0].wait()
    posT[...] = pos[...].T
    loads[1].wait()
    tail = jnp.concatenate([jnp.ones((1, VIS), BF), jnp.zeros((EXT - HS - 1, VIS), BF)], axis=0)
    vtail = jnp.concatenate([jnp.ones((VIS, 2), BF), jnp.zeros((VIS, EXT - HS - 2), BF)], axis=1)
    for l in range(2):
        keys = nn(nf[l], kw[l, :, 0:DD]).astype(BF)
        vals = nn(nf[l], kw[l, :, DD:2 * DD]).astype(BF)
        kT[l] = keys.T
        vT = vals.T
        for h in range(HEADS):
            hs = slice(h * HS, (h + 1) * HS)
            k2[l, h] = jnp.concatenate([keys[:, hs], keys[:, hs]], axis=1)
            vx[l, h] = jnp.concatenate([vals[:, hs], vtail], axis=1)
            vTx[l, h] = jnp.concatenate([vT[hs, :], tail], axis=0)
    keep = [
        pltpu.make_async_copy(kT.at[0], kT_hbm, ksem.at[0]),
        pltpu.make_async_copy(vx.at[0], vx_hbm, ksem.at[1]),
        pltpu.make_async_copy(nfT.at[0], nfT_hbm, ksem.at[2]),
    ]
    for cp in keep:
        cp.start()
    dkvT[...] = jnp.zeros_like(dkvT)
    esum[...] = jnp.zeros_like(esum)

    def fwd_layer(l, x, t0, w):
        tsl = pl.ds(t0, w)
        n, r = norm(x, wide(gains[l], w))
        nq[l, :, tsl] = n
        rs[l, :, tsl] = r
        qb = nn(qwT[l], n).astype(BF)
        qs[l, :, tsl] = qb
        qf = qb.astype(F32) * LOG2
        hi = qf.astype(BF)
        lo = (qf - hi.astype(F32)).astype(BF)
        q2[:, 0:HS, 0:w] = hi.reshape(HEADS, HS, w)
        q2[:, HS:2 * HS, 0:w] = lo.reshape(HEADS, HS, w)

        def scores(h):
            return nn(k2[l, h], q2[h, :, 0:w])

        def soft(h, s):
            p = jnp.exp2(s - jnp.max(s, axis=0, keepdims=True)).astype(BF)
            if l == 0:
                probs0[h, :, tsl] = p
            else:
                probs1[h, :, 0:w] = p
            return p

        def mix(h, p):
            o = nn(vTx[l, h], p)
            inv = 1.0 / o[HS:HS + 1]
            invs[l, h:h + 1, tsl] = inv
            ms[l, h * HS:(h + 1) * HS, tsl] = (o[:HS] * inv).astype(BF)

        n_g = HEADS // GF
        s = [scores(u) for u in range(GF)]
        before = None
        for g in range(n_g):
            s2 = [scores((g + 1) * GF + u) for u in range(GF)] if g + 1 < n_g else None
            ps = [soft(g * GF + u, s[u]) for u in range(GF)]
            if before is not None:
                for u in range(GF):
                    mix((g - 1) * GF + u, before[u])
            s, before = s2, ps
        for u in range(GF):
            mix((n_g - 1) * GF + u, before[u])
        return x + nn(owT[l], ms[l, :, tsl])

    def chunk_out(i, t0, w):
        tsl = pl.ds(t0, w)
        pairs = (
            (nq.at[0, :, tsl], nq_hbm.at[:, tsl]), (qs.at[0, :, tsl], qs_hbm.at[:, tsl]),
            (ms.at[0, :, tsl], ms_hbm.at[:, tsl]), (dus.at[0, :, tsl], dus_hbm.at[:, tsl]),
            (probs0.at[:, :, tsl], probs_hbm.at[:, :, tsl]), (invs.at[0, :, tsl], invs_hbm.at[:, tsl]))
        return [pltpu.make_async_copy(a, b, csem.at[k, i]) for k, (a, b) in enumerate(pairs)]

    def chunk_a(i, t0, w, span):
        tsl = pl.ds(t0, w)
        low = pl.multiple_of(t0 // MASKED * SPATIAL // 128 * 128, 128)
        ids = idx_ref[:, tsl] - low
        onehot = (lax.broadcasted_iota(jnp.int32, (span, w), 0) == ids).astype(BF)
        x = wide(gains[3], w) + nn(posT[:, pl.ds(low, span)], onehot)
        x = fwd_layer(0, x, t0, w)
        x = fwd_layer(1, x, t0, w)
        n, r = norm(x, wide(gains[2], w))
        no[:, tsl] = n
        nT = n.T
        e = nn(nT, hw[...]) - err[tsl, :].astype(F32)
        esum[...] += jnp.sum(e * e, axis=0, keepdims=True)
        eb = e.astype(BF)
        err[tsl, :] = eb
        dn = nt(hw[...], eb)
        dx = norm_back(dn, n, r, wide(gains[2], w))
        du = dx.astype(BF)
        dus[1, :, tsl] = du
        attention_back(du, w, tsl, ow.at[1], invs.at[1], ms.at[1], lambda h: probs1[h, :, 0:w], vx.at[1], kT.at[1],
                       qs.at[1], dme, dqs, dkvT)
        dn = nn(qw[1], dqs[:, tsl])
        dx = dx + norm_back(dn, nq[1, :, tsl], rs[1, :, tsl], wide(gains[1], w))
        dus[0, :, tsl] = dx.astype(BF)
        for cp in chunk_out(i, t0, w):
            cp.start()

    full = ROWS // WIDE
    rem = ROWS - full * WIDE
    frames = 1 + -(-(WIDE - 1) // MASKED)

    @pl.loop(0, full)
    def _(i):
        @pl.when(i == 0)
        def _():
            loads[4].wait()
            loads[5].wait()

        chunk_a(i, pl.multiple_of(i * WIDE, WIDE), WIDE, -(-(frames * SPATIAL + 127) // 128) * 128)

    chunk_a(full, full * WIDE, rem, TOKS - full * WIDE // MASKED * SPATIAL // 128 * 128)

    loss_ref[...] = jnp.full((8, 128), jnp.sum(esum[...]), F32)
    emit, finish = make_emit(stage, gsem)
    for b in range(2):
        to = pl.ds(64 * b, 64)
        emit(nn, no[b * 256:(b + 1) * 256, :], lambda c: err[:, c:c + 256], 256, PIX, 48, [
            (0, 40, g1_hbm.at[to, pl.ds(24, 40)]), (40, 48, g2_hbm.at[to, pl.ds(32, 8)])])
    emit(nt, nq[1], lambda c: dqs[c:c + 256, :], DD, DD, 16, [(0, 16, g2_hbm.at[:, pl.ds(0, 16)])])
    emit(nt, ms[1], lambda c: dus[1, c:c + 256, :], DD, DD, 16, [(0, 16, g2_hbm.at[:, pl.ds(16, 16)])])
    dT[0:DD, :] = (dkvT[0:DD, :] * SCALE).astype(BF)
    dT[DD:2 * DD, :] = dkvT[DD:2 * DD, :].astype(BF)
    keep.append(pltpu.make_async_copy(dT, d_hbm, ksem.at[3]))
    keep[3].start()
    for b in range(4):
        to = pl.ds(32 * b, 32)
        emit(nt, nfT[1, b * 352:(b + 1) * 352, :], lambda c: dT[c:c + 256, :], 352, 2 * DD, 88, [
            (0, 64, g0_hbm.at[to, pl.ds(0, 64)]), (64, 88, g1_hbm.at[to, pl.ds(0, 24)])])
    finish()
    for cp in keep:
        cp.wait()

    for i in range(full + 1):
        for cp in chunk_out(i, i * WIDE, min(WIDE, ROWS - i * WIDE)):
            cp.wait()


ROWS_1 = (64, 64, 40)
ROWS_2 = (32, 32, 56)


def compute(features, masked_index, pos_table, mask_token, key_gain, key_weight, query_gain,
            query_weight, out_weight, out_gain, head_weight, target):
    vm = pl.BlockSpec(memory_space=pltpu.VMEM)
    hb = pl.BlockSpec(memory_space=pl.ANY)
    S = jax.ShapeDtypeStruct
    out_shape = (
        S((8, 128), F32), *(S((128, r, 128), F32) for r in ROWS_1),
        S((DD, ROWS), BF), S((DD, ROWS), BF), S((DD, ROWS), BF), S((DD, ROWS), BF),
        S((HEADS, VIS, ROWS), BF), S((HEADS, ROWS), F32),
        S((DD, VIS), BF), S((HEADS, VIS, EXT), BF), S((D, VIS), BF), S((2 * DD, VIS), BF),
    )
    V = pltpu.VMEM
    scratch = [
        V((TOKS, DD), BF), V((2, D, 2 * DD), BF), V((2, DD, DD), BF), V((2, DD, DD), BF), V((DD, PIX), BF),
        V((ROWS, PIX), BF), V((DD, TOKS), BF), V((2, DD, DD), BF), V((2, DD, DD), BF),
        V((2, VIS, D), BF), V((2, D, VIS), BF),
        V((2, HEADS, VIS, 2 * HS), BF), V((2, HEADS, VIS, EXT), BF), V((2, HEADS, EXT, VIS), BF), V((2, DD, VIS), BF),
        V((HEADS, VIS, ROWS), BF), V((HEADS, VIS, WIDE), BF),
        V((2, DD, ROWS), BF), V((2, DD, ROWS), BF), V((2, DD, ROWS), BF), V((2, DD, ROWS), BF), V((DD, ROWS), BF),
        V((DD, ROWS), BF), V((2, 1, ROWS), F32), V((2, HEADS, ROWS), F32), V((2 * DD, VIS), F32),
        V((4, DD, 128), F32), V((HEADS, 2 * HS, WIDE), BF), V((HEADS, EXT, WIDE), BF),
        V((2, SLOT, 128), F32), V((1, PIX), F32), V((2 * DD, VIS), BF),
        pltpu.SemaphoreType.DMA((6,)), pltpu.SemaphoreType.DMA((2, 3)), pltpu.SemaphoreType.DMA((6, NCH)),
        pltpu.SemaphoreType.DMA((4,)),
    ]
    return pl.pallas_call(
        compute_kernel,
        out_shape=out_shape,
        in_specs=[vm] * 6 + [hb] * 6,
        out_specs=[vm] + [hb] * 13,
        scratch_shapes=scratch,
        compiler_params=pltpu.CompilerParams(vmem_limit_bytes=63 * 1024 * 1024),
        name="decode",
    )(
        masked_index, features, mask_token, key_gain, query_gain, out_gain,
        pos_table, key_weight, query_weight, out_weight, head_weight, target,
    )


MESH = pl.DeviceIdType.MESH
PARTS = 3
ORDERS = (("x", "y", "z"), ("y", "z", "x"), ("z", "x", "y"))


def part_index(coords):
    y = coords["y"]
    if isinstance(y, slice):
        return (y, coords["x"], coords["z"], y)
    return (y // 2, coords["x"], coords["z"], y % 2)


def block_shape(free):
    shape = []
    for name, size in (("y", 2), ("x", 4), ("z", 4), ("y", 2)):
        if name in free:
            shape.append(size)
    return tuple(shape)


def reduce_kernel(
    loss_ref, kgain_ref, feat_hbm,
    g0, g1, g2, nq_hbm, qs_hbm, ms_hbm, dus_hbm, probs_hbm, invs_hbm, kT_hbm, vx_hbm, nfT_hbm, d_hbm, ow_hbm, kw_hbm,
    k_out, q_out, o_out, h_out, l_out, fgrad_hbm,
    feat_ref, nq, qs, ms, dus, probs0, invs, kT, vx, nfT, d1, ow, kw, dqs, dkvT, dT, dme, stage, lbuf,
    send, recv, lsem, csem, ksem, gsem, *rest,
):
    own1, own2, got1, got2 = (rest[3 * i:3 * i + 3] for i in range(4))
    buffers = rest[12:]
    clip, tok = lax.axis_index("clip"), lax.axis_index("tok")
    me = {"x": clip % 4, "y": (clip // 4) * 2 + (tok // 2) % 2, "z": tok // 4}
    core = tok % 2
    full_slice = slice(None)

    def device(c, k):
        return ((c["y"] // 2) * 4 + c["x"], c["z"] * 4 + (c["y"] % 2) * 2 + k)

    def shifted(axis, by):
        c = dict(me)
        c[axis] = (me[axis] + by + 4) % 4
        return c

    partner = device(me, 1 - core)
    sides = {a: tuple(device(shifted(a, by), core) for by in (1, -1, 2)) for a in "xyz"}

    chunks = [(i * CH, min(CH, ROWS - i * CH)) for i in range(NCH)]

    def chunk_in(i, t0, w):
        tsl = pl.ds(t0, w)
        pairs = (
            (dus_hbm.at[:, tsl], dus.at[:, tsl]), (invs_hbm.at[:, tsl], invs.at[:, tsl]),
            (ms_hbm.at[:, tsl], ms.at[:, tsl]), (probs_hbm.at[:, :, tsl], probs0.at[:, :, tsl]),
            (qs_hbm.at[:, tsl], qs.at[:, tsl]), (nq_hbm.at[:, tsl], nq.at[:, tsl]))
        return [pltpu.make_async_copy(a, b, csem.at[k, i]) for k, (a, b) in enumerate(pairs)]

    others = [
        pltpu.make_async_copy(ow_hbm.at[0], ow, ksem.at[0]), pltpu.make_async_copy(vx_hbm, vx, ksem.at[1]),
        pltpu.make_async_copy(kT_hbm, kT, ksem.at[2]), pltpu.make_async_copy(nfT_hbm, nfT, ksem.at[3]),
        pltpu.make_async_copy(d_hbm, d1, ksem.at[4]), pltpu.make_async_copy(kw_hbm, kw, ksem.at[5]),
        pltpu.make_async_copy(feat_hbm, feat_ref, ksem.at[6])]
    for cp in others[0:3]:
        cp.start()
    for cp in chunk_in(0, 0, CH):
        cp.start()

    barrier = pltpu.get_barrier_semaphore()
    for dev in [partner] + [d for a in "xyz" for d in sides[a]]:
        pl.semaphore_signal(barrier, inc=1, device_id=dev, device_id_type=MESH)
    pl.semaphore_wait(barrier, 10)

    counter = [0]

    def remote(src, dst, dev):
        i = counter[0]
        counter[0] += 1
        return pltpu.make_async_remote_copy(
            src_ref=src, dst_ref=dst, send_sem=send.at[i], recv_sem=recv.at[i], device_id=dev, device_id_type=MESH)

    class Group:
        def __init__(self, srcs, owns, gots, own_index, bufs, base):
            self.srcs, self.owns, self.gots, self.own_index = srcs, owns, gots, own_index
            self.first, self.second = bufs[0:6], bufs[6:15]
            self.swaps, self.mine = {}, {}
            k = base
            for by in (2, 1, 3, 0):
                for p in range(PARTS):
                    i = part_index(self.coords(p, 0, self.at(p, 0, by)))
                    self.swaps[p, by] = remote(srcs[p].at[i + (1 - core,)], gots[p].at[i], partner)
                    if base is not None:
                        self.mine[p, by] = pltpu.make_async_copy(srcs[p].at[i + (core,)], owns[p].at[i], lsem.at[k])
                        k += 1
            self.far, self.early, self.late, self.direct = {}, {}, {}, {}
            for p in range(PARTS):
                for s in range(2):
                    right, left = sides[ORDERS[p][s]][:2]
                    f, o = self.first[s * 3 + p], self.second[s * 3 + p]
                    lo, hi = self.halves(p, s)
                    self.far[s, p] = (
                        remote(self.block(p, s, 2, lo), f.at[lo], right), remote(self.block(p, s, 2, hi), f.at[hi], left))
                    self.early[s, p] = (
                        remote(self.block(p, s, 1, hi), o.at[0, hi], right),
                        remote(self.block(p, s, 3, lo), o.at[1, lo], left))
                    self.late[s, p] = (
                        remote(self.block(p, s, 1, lo), o.at[0, lo], right),
                        remote(self.block(p, s, 3, hi), o.at[1, hi], left))
                right, left, across = sides[ORDERS[p][2]]
                o = self.second[6 + p]
                self.direct[2, p] = tuple(
                    remote(self.block(p, 2, by), o.at[i], dev) for i, (by, dev) in enumerate(((1, right), (3, left), (2, across))))

        def halves(self, p, s):
            n = block_shape(ORDERS[p][s + 1:])[0]
            return slice(0, n // 2), slice(n // 2, n)

        def at(self, p, s, by):
            return (me[ORDERS[p][s]] + by) % 4

        def coords(self, p, s, j):
            c = {}
            for t, a in enumerate(ORDERS[p]):
                c[a] = me[a] if t < s else (j if t == s else full_slice)
            return c

        def index(self, p, s, by, half=None):
            out = list(part_index(self.coords(p, s, self.at(p, s, by))))
            if half is not None:
                out[[isinstance(i, slice) for i in out].index(True)] = half
            return tuple(out) + self.own_index

        def block(self, p, s, by, half=None):
            return self.owns[p].at[self.index(p, s, by, half)]

        def swap(self, *places):
            for by in places:
                for p in range(PARTS):
                    self.swaps[p, by].start()
                    if self.mine:
                        self.mine[p, by].start()

        def add_swap(self, by):
            for p in range(PARTS):
                if self.mine:
                    self.mine[p, by].wait()
                self.swaps[p, by].wait_recv()

                i = self.index(p, 0, by)
                self.owns[p][i] = self.owns[p][i] + self.gots[p][i[:4]]

        def send_far(self, s):
            for p in range(PARTS):
                for cp in self.far[s, p]:
                    cp.start()

        def send_early(self, s):
            for p in range(PARTS):
                for cp in self.early[s, p]:
                    cp.start()

        def send_late(self, s):
            for p in range(PARTS):
                for cp in self.far[s, p]:
                    cp.wait_recv()
                lo, hi = self.halves(p, s)
                r, l = self.index(p, s, 1, lo), self.index(p, s, 3, hi)
                own, f = self.owns[p], self.first[s * 3 + p]
                own[r] = own[r] + f[lo]
                own[l] = own[l] + f[hi]
                for cp in self.late[s, p]:
                    cp.start()

        def collect(self, s):
            for p in range(PARTS):
                for cp in self.early[s, p] + self.late[s, p]:
                    cp.wait_recv()
                own, o = self.owns[p], self.second[s * 3 + p]
                m = self.index(p, s, 0)
                own[m] = own[m] + o[0] + o[1]

        def send_direct(self):
            for p in range(PARTS):
                for cp in self.direct[2, p]:
                    cp.start()

        def collect_direct(self):
            for p in range(PARTS):
                for cp in self.direct[2, p]:
                    cp.wait_recv()
                own, o = self.owns[p], self.second[6 + p]
                m = self.index(p, 2, 0)
                own[m] = own[m] + o[0] + o[1] + o[2]

        def finish(self):
            for cp in self.swaps.values():
                cp.wait_send()
            for sent in (self.far, self.early, self.late, self.direct):
                for cps in sent.values():
                    for cp in cps:
                        cp.wait_send()

    one = Group((g0, g1, g2), own1, got1, (), buffers[0:15], 0)
    two = Group(own2, own2, got2, (core,), buffers[15:30], None)

    one.swap(2, 1, 3, 0)
    for i, (t0, w) in enumerate(chunks[1:]):
        for cp in chunk_in(i + 1, t0, w):
            cp.start()
    for cp in others[3:]:
        cp.start()
    lbuf[0, core] = loss_ref[...]
    lcopy = remote(loss_ref, lbuf.at[0, core], partner)
    lcopy.start()

    l_near, l_far = [], []
    for s, axis in enumerate("xyz"):
        mine = lbuf.at[s + 1, me[axis]]
        l_near.append([remote(mine, mine, sides[axis][0]), remote(mine, mine, sides[axis][1])])
        far = lbuf.at[s + 1, (me[axis] + 3) % 4]
        l_far.append(remote(far, far, sides[axis][0]))

    def loss_near(s):
        if s == 0:
            lcopy.wait()
            tile = lbuf[0, 0] + lbuf[0, 1]
        else:
            l_far[s - 1].wait()
            tile = lbuf[s, 0] + lbuf[s, 1] + lbuf[s, 2] + lbuf[s, 3]
        lbuf[s + 1, me["xyz"[s]]] = tile
        for cp in l_near[s]:
            cp.start()

    def loss_far(s):
        for cp in l_near[s]:
            cp.wait()
        l_far[s].start()

    dkvT[...] = jnp.zeros_like(dkvT)
    for cp in others[0:3]:
        cp.wait()

    def chunk_b(i, t0, w):
        tsl = pl.ds(t0, w)
        for cp in chunk_in(i, t0, w):
            cp.wait()
        attention_back(dus[:, tsl], w, tsl, ow, invs, ms, lambda h: probs0[h, :, tsl], vx, kT, qs, dme, dqs, dkvT)

    @pl.loop(0, ROWS // CH)
    def _(i):
        chunk_b(i, pl.multiple_of(i * CH, CH), CH)

        @pl.when(i == 1)
        def _():
            one.add_swap(2)
            one.send_far(0)
            loss_near(0)

        @pl.when(i == 3)
        def _():
            one.add_swap(1)
            one.add_swap(3)
            one.send_early(0)

    chunk_b(NCH - 1, *chunks[NCH - 1])
    one.send_late(0)
    loss_far(0)
    one.add_swap(0)

    emit, flush = make_emit(stage, gsem)
    flat = [o.reshape(128, r, 128) for o, r in zip(own2, ROWS_2)]
    emit(nt, nq[...], lambda c: dqs[c:c + 256, :], DD, DD, 16, [(0, 16, flat[2].at[:, pl.ds(24, 16)])])
    emit(nt, ms[...], lambda c: dus[c:c + 256, :], DD, DD, 16, [(0, 16, flat[2].at[:, pl.ds(40, 16)])])
    dT[0:DD, :] = (dkvT[0:DD, :] * SCALE).astype(BF)
    dT[DD:2 * DD, :] = dkvT[DD:2 * DD, :].astype(BF)
    others[3].wait()
    for b in range(4):
        to = pl.ds(32 * b, 32)
        emit(nt, nfT[b * 352:(b + 1) * 352, :], lambda c: dT[c:c + 256, :], 352, 2 * DD, 88, [
            (0, 32, flat[0].at[to]), (32, 64, flat[1].at[to]), (64, 88, flat[2].at[to, pl.ds(0, 24)])])
    flush()
    two.swap(2, 1, 3, 0)

    def feature_grad(l, d):
        dn = nt(d.T, kw[l])
        xh, r = feature_norm(feat_ref, l)
        dxh = dn * kgain_ref[l:l + 1, :].astype(F32)
        m1 = jnp.mean(dxh, axis=1, keepdims=True)
        m2 = jnp.mean(dxh * xh, axis=1, keepdims=True)
        feat_ref[l] = (r * (dxh - m1 - xh * m2)).astype(BF)

    for cp in others[4:]:
        cp.wait()
    two.add_swap(2)
    two.send_far(0)
    two.add_swap(1)
    two.add_swap(3)
    two.send_early(0)
    one.collect(0)
    one.send_far(1)
    one.send_early(1)
    loss_near(1)
    feature_grad(0, dT[...])
    feature_grad(1, d1[...])
    f_copy = pltpu.make_async_copy(feat_ref, fgrad_hbm, ksem.at[7])
    f_copy.start()
    two.add_swap(0)
    two.send_late(0)
    one.send_late(1)
    loss_far(1)
    one.collect(1)
    one.send_direct()
    loss_near(2)
    two.collect(0)
    two.send_far(1)
    two.send_early(1)
    loss_far(2)
    one.collect_direct()
    two.send_late(1)
    l_far[2].wait()
    l_out[...] = lbuf[3, 0] + lbuf[3, 1] + lbuf[3, 2] + lbuf[3, 3]
    two.collect(1)
    two.send_direct()

    at = part_index(me)

    def rows(group, p, start, n, stride=1):
        own = own1 if group == 1 else own2
        ix = at if group == 1 else at + (core,)
        return own[p][ix + ((pl.ds(start, n, stride=stride)),)] if stride > 1 else own[p][ix + (pl.ds(start, n),)]

    for j in range(8):
        k_out[1, 0:8, j * 128:(j + 1) * 128] = rows(1, 0, j, 8, 8)
        k_out[1, 8:11, j * 128:(j + 1) * 128] = rows(1, 1, j, 3, 8)
    for j in range(4):
        q_out[1, :, j * 128:(j + 1) * 128] = rows(1, 2, j, 4, 4)
        o_out[1, :, j * 128:(j + 1) * 128] = rows(1, 2, 16 + j, 4, 4)
    for r in range(4):
        for j in range(12):
            i = r * 12 + j
            h_out[r:r + 1, j * 128:(j + 1) * 128] = rows(1, 1, 24 + i, 1) if i < 40 else rows(1, 2, i - 8, 1)
    two.collect_direct()
    for j in range(8):
        lanes = slice(j * 128, (j + 1) * 128)
        k_out[0, 0:4, lanes] = rows(2, 0, j, 4, 8)
        k_out[0, 4:8, lanes] = rows(2, 1, j, 4, 8)
        k_out[0, 8:11, lanes] = rows(2, 2, j, 3, 8)
    for j in range(4):
        lanes = slice(j * 128, (j + 1) * 128)
        q_out[0, :, lanes] = rows(2, 2, 24 + j, 4, 4)
        o_out[0, :, lanes] = rows(2, 2, 40 + j, 4, 4)
    one.finish()
    two.finish()
    f_copy.wait()


def reduce_scatter(state, features, key_gain, key_weight, out_weight):
    V = pltpu.VMEM
    vm = pl.BlockSpec(memory_space=pltpu.VMEM)
    hb = pl.BlockSpec(memory_space=pl.ANY)
    S = jax.ShapeDtypeStruct
    loss, parts, rest = state[0], state[1:4], state[4:]
    grid = (2, 4, 4, 2)
    scratch = [
        V((2, VIS, D), BF),
        V((DD, ROWS), BF), V((DD, ROWS), BF), V((DD, ROWS), BF), V((DD, ROWS), BF),
        V((HEADS, VIS, ROWS), BF), V((HEADS, ROWS), F32),
        V((DD, VIS), BF), V((HEADS, VIS, EXT), BF), V((D, VIS), BF), V((2 * DD, VIS), BF),
        V((DD, DD), BF), V((2, D, 2 * DD), BF), V((DD, ROWS), BF), V((2 * DD, VIS), F32), V((2 * DD, VIS), BF),
        V((HEADS, EXT, CH), BF), V((2, SLOT, 128), F32), V((4, 4, 8, 128), F32),
    ]
    n_copies = 2 * (12 + 36 + 9) + 1 + 9
    dma = pltpu.SemaphoreType.DMA
    scratch += [dma((n_copies,)), dma((n_copies,)), dma((12,)), dma((6, NCH)), dma((8,)), dma((2, 3))]
    scratch += [V(grid + (r, 128), F32) for r in ROWS_1] + [V(grid + (2, r, 128), F32) for r in ROWS_2]
    scratch += [V(grid + (r, 128), F32) for r in ROWS_1] + [V(grid + (r, 128), F32) for r in ROWS_2]
    for rows in (ROWS_1, ROWS_2):
        for n, stages in (((), (0, 1)), ((2,), (0, 1)), ((3,), (2,))):
            for s in stages:
                for p in range(PARTS):
                    scratch.append(V(n + block_shape(ORDERS[p][s + 1:]) + (rows[p], 128), F32))
    return pl.pallas_call(
        reduce_kernel,
        out_shape=(
            S((2, 11, 2 * DD), F32), S((2, 4, DD), F32), S((2, 4, DD), F32), S((4, PIX), F32), S((8, 128), F32),
            S((2, VIS, D), BF),
        ),
        in_specs=[vm] * 2 + [hb] * 16,
        out_specs=[vm] * 5 + [hb],
        scratch_shapes=scratch,
        compiler_params=pltpu.CompilerParams(
            collective_id=0, has_side_effects=True, vmem_limit_bytes=63 * 1024 * 1024),
        name="reduce",
    )(
        loss, key_gain, features, *(g.reshape(grid + (2,) + g.shape[1:]) for g in parts), *rest, out_weight, key_weight)


def output_kernel(loss, k_in, q_in, o_in, h_in, f_in, loss_out, k_out, q_out, o_out, h_out, f_out):
    loss_out[0, 0] = loss[0, 0] * (1.0 / (128 * ROWS * PIX))
    for l in range(2):
        k_out[:, l, :] = k_in[l]
    for a, b in ((f_in, f_out), (q_in, q_out), (o_in, o_out), (h_in, h_out)):
        b[...] = a[...]


def outputs(k, q, o, h, loss, f):
    vm = pl.BlockSpec(memory_space=pltpu.VMEM)
    sm = pl.BlockSpec(memory_space=pltpu.SMEM)
    arrays = (k, q, o, h, f)
    return pl.pallas_call(
        output_kernel,
        out_shape=(jax.ShapeDtypeStruct((1, 1), F32), jax.ShapeDtypeStruct((11, 2, 2 * DD), F32),
                   *(jax.ShapeDtypeStruct(a.shape, a.dtype) for a in arrays[1:])),
        in_specs=[sm] + [vm] * 5,
        out_specs=[sm] + [vm] * 5,
        name="outputs",
    )(loss, *arrays)


def shards(features, masked_index, pos_table, mask_token, key_gain, key_weight, query_gain,
           query_weight, out_weight, out_gain, head_weight, target):
    state = compute(
        features, masked_index, pos_table, mask_token, key_gain, key_weight, query_gain,
        query_weight, out_weight, out_gain, head_weight, target)
    summed = reduce_scatter(state, features, key_gain, key_weight, out_weight)
    loss, key_grad, query_grad, out_grad, head_grad, feature_grad = outputs(*summed)
    return loss[0, 0], feature_grad, key_grad.transpose(1, 0, 2), query_grad, out_grad, head_grad


def solution(mesh):
    both = ("clip", "tok")
    in_specs = (
        P(None, both, None), P(both, None), P(), P(), P(), P(), P(), P(), P(), P(), P(), P(both, None, None))
    out_specs = (
        P(), P(None, both, None), P(None, both, None), P(None, both, None), P(None, both, None), P(both, None))
    return jax.shard_map(shards, mesh=mesh, in_specs=in_specs, out_specs=out_specs, check_vma=False)
```

```python
import math

import jax
import jax.numpy as jnp
from jax import lax
from jax.experimental import pallas as pl
from jax.experimental.pallas import tpu as pltpu
from jax.sharding import PartitionSpec as P

HEADS = 16
HS = 32
VIS = 160
D = 1408
DD = 512
PIX = 1536
ROWS = 1408
TOKS = 1568
CH = 256
WIDE = 512
EXT = 48
EPS = 1e-6
F32 = jnp.float32
BF = jnp.bfloat16
SCALE = 1.0 / math.sqrt(HS)
LOG2 = SCALE * math.log2(math.e)
GF = 4
GB = 2
SLOT = 3072
NCH = 6
SPATIAL = 196
MASKED = 176


def nn(a, b):
    return lax.dot_general(a, b, (((1,), (0,)), ((), ())), preferred_element_type=F32)


def nt(a, b):
    return lax.dot_general(a, b, (((1,), (1,)), ((), ())), preferred_element_type=F32)


def wide(g, w):
    return jnp.concatenate([g] * (w // 128), axis=1)


def norm(x, gain):
    c = x - jnp.mean(x, axis=0, keepdims=True)
    r = lax.rsqrt(jnp.mean(c * c, axis=0, keepdims=True) + EPS)
    return (c * r * gain).astype(BF), r


def norm_back(dy, n, r, gain):
    n = n.astype(F32)
    m2 = jnp.mean(dy * n, axis=0, keepdims=True)
    dxh = dy * gain
    m1 = jnp.mean(dxh, axis=0, keepdims=True)
    return r * (dxh - m1 - n * (m2 / gain))


def feature_norm(feat_ref, l):
    f = feat_ref[l].astype(F32)
    c = f - jnp.mean(f, axis=1, keepdims=True)
    r = lax.rsqrt(jnp.mean(c * c, axis=1, keepdims=True) + EPS)
    return c * r, r


def attention_back(du, w, tsl, ow, invs, ms, probs, vx, kT, qs, dme, dqs, dkvT):
    dm = nn(ow[...], du).reshape(HEADS, HS, w) * invs[:, tsl].reshape(HEADS, 1, w)
    dm = dm.astype(BF)
    dme[:, 0:HS, 0:w] = dm
    dsum = jnp.sum(dm.astype(F32) * ms[:, tsl].astype(F32).reshape(HEADS, HS, w), axis=1, keepdims=True)
    hi = dsum.astype(BF)
    lo = (dsum - hi.astype(F32)).astype(BF)
    dme[:, HS:EXT, 0:w] = jnp.concatenate([-hi, -lo, jnp.zeros((HEADS, EXT - HS - 2, w), BF)], axis=1)

    def dprobs(h):
        return nn(vx[h], dme[h, :, 0:w])

    def dscores(h, x):
        return (probs(h).astype(F32) * x).astype(BF)

    def rest(h, ds):
        hs = slice(h * HS, (h + 1) * HS)
        vs = slice(DD + h * HS, DD + (h + 1) * HS)
        dqs[hs, tsl] = (nn(kT[hs, :], ds) * SCALE).astype(BF)
        dkvT[hs, :] += nt(qs[hs, tsl], ds)
        dkvT[vs, :] += nt(dme[h, 0:HS, 0:w], probs(h))

    n_g = HEADS // GB
    x = [dprobs(u) for u in range(GB)]
    before = None
    for g in range(n_g):
        x2 = [dprobs((g + 1) * GB + u) for u in range(GB)] if g + 1 < n_g else None
        ds = [dscores(g * GB + u, x[u]) for u in range(GB)]
        if before is not None:
            for u in range(GB):
                rest((g - 1) * GB + u, before[u])
        x, before = x2, ds
    for u in range(GB):
        rest((n_g - 1) * GB + u, before[u])


def make_emit(stage, gsem):
    pending = [[], []]
    count = [0]

    def emit(dot, lhs, rhs, rows, width, share, dsts):
        slot = count[0] % 2
        count[0] += 1
        for cp in pending[slot]:
            cp.wait()
        parts = width // 128
        for c in range(width // 256):
            block = dot(lhs, rhs(c * 256))
            for j in range(2):
                stage[slot, pl.ds(2 * c + j, rows, stride=parts), :] = block[:, j * 128:(j + 1) * 128]
        n = rows * parts
        src = stage.at[slot, pl.ds(0, n)].reshape(n // share, share, 128)
        pending[slot] = []
        for i, (lo, hi, dst) in enumerate(dsts):
            cp = pltpu.make_async_copy(src.at[:, pl.ds(lo, hi - lo)], dst, gsem.at[slot, i])
            cp.start()
            pending[slot].append(cp)

    def finish():
        for cp in pending[0] + pending[1]:
            cp.wait()
        pending[0], pending[1] = [], []

    return emit, finish


def compute_kernel(
    idx_ref, feat_ref, tok_ref, kgain_ref, qgain_ref, ogain_ref,
    pos_hbm, kw_hbm, qw_hbm, ow_hbm, hw_hbm, tgt_hbm,
    loss_ref, g0_hbm, g1_hbm, g2_hbm, nq_hbm, qs_hbm, ms_hbm, dus_hbm, probs_hbm, invs_hbm,
    kT_hbm, vx_hbm, nfT_hbm, d_hbm,
    pos, kw, qw, ow, hw, err, posT, qwT, owT, nf, nfT, k2, vx, vTx, kT, probs0, probs1,
    nq, qs, ms, dus, dqs, no, rs, invs, dkvT, gains, q2, dme, stage, esum, dT, sems, gsem, csem, ksem,
):
    loads = [
        pltpu.make_async_copy(pos_hbm, pos, sems.at[0]),
        pltpu.make_async_copy(kw_hbm, kw, sems.at[1]),
        pltpu.make_async_copy(qw_hbm, qw, sems.at[2]),
        pltpu.make_async_copy(ow_hbm, ow, sems.at[3]),
        pltpu.make_async_copy(hw_hbm, hw, sems.at[4]),
        pltpu.make_async_copy(tgt_hbm.at[0], err, sems.at[5]),
    ]
    for i in (2, 3, 0, 1):
        loads[i].start()

    for i, row in enumerate((qgain_ref[0:1, :], qgain_ref[1:2, :], ogain_ref[...], tok_ref[...])):
        gains[i] = jnp.broadcast_to(row.astype(F32).reshape(1, DD), (128, DD)).T

    for l in range(2):
        n = (feature_norm(feat_ref, l)[0] * kgain_ref[l:l + 1, :].astype(F32)).astype(BF)
        nf[l] = n
        nfT[l] = n.T
    loads[2].wait()
    loads[3].wait()
    for l in range(2):
        qwT[l] = qw[l].T
        owT[l] = ow[l].T
    loads[0].wait()
    posT[...] = pos[...].T
    loads[1].wait()
    loads[4].start()
    loads[5].start()
    tail = jnp.concatenate([jnp.ones((1, VIS), BF), jnp.zeros((EXT - HS - 1, VIS), BF)], axis=0)
    vtail = jnp.concatenate([jnp.ones((VIS, 2), BF), jnp.zeros((VIS, EXT - HS - 2), BF)], axis=1)
    for l in range(2):
        keys = nn(nf[l], kw[l, :, 0:DD]).astype(BF)
        vals = nn(nf[l], kw[l, :, DD:2 * DD]).astype(BF)
        kT[l] = keys.T
        vT = vals.T
        for h in range(HEADS):
            hs = slice(h * HS, (h + 1) * HS)
            k2[l, h] = jnp.concatenate([keys[:, hs], keys[:, hs]], axis=1)
            vx[l, h] = jnp.concatenate([vals[:, hs], vtail], axis=1)
            vTx[l, h] = jnp.concatenate([vT[hs, :], tail], axis=0)
    keep = [
        pltpu.make_async_copy(kT.at[0], kT_hbm, ksem.at[0]),
        pltpu.make_async_copy(vx.at[0], vx_hbm, ksem.at[1]),
        pltpu.make_async_copy(nfT.at[0], nfT_hbm, ksem.at[2]),
    ]
    for cp in keep:
        cp.start()
    dkvT[...] = jnp.zeros_like(dkvT)
    esum[...] = jnp.zeros_like(esum)

    def fwd_layer(l, x, t0, w):
        tsl = pl.ds(t0, w)
        n, r = norm(x, wide(gains[l], w))
        nq[l, :, tsl] = n
        rs[l, :, tsl] = r
        qb = nn(qwT[l], n).astype(BF)
        qs[l, :, tsl] = qb
        qf = qb.astype(F32) * LOG2
        hi = qf.astype(BF)
        lo = (qf - hi.astype(F32)).astype(BF)
        q2[:, 0:HS, 0:w] = hi.reshape(HEADS, HS, w)
        q2[:, HS:2 * HS, 0:w] = lo.reshape(HEADS, HS, w)

        def scores(h):
            return nn(k2[l, h], q2[h, :, 0:w])

        def soft(h, s):
            p = jnp.exp2(s - jnp.max(s, axis=0, keepdims=True)).astype(BF)
            if l == 0:
                probs0[h, :, tsl] = p
            else:
                probs1[h, :, 0:w] = p
            return p

        def mix(h, p):
            o = nn(vTx[l, h], p)
            inv = 1.0 / o[HS:HS + 1]
            invs[l, h:h + 1, tsl] = inv
            ms[l, h * HS:(h + 1) * HS, tsl] = (o[:HS] * inv).astype(BF)

        n_g = HEADS // GF
        s = [scores(u) for u in range(GF)]
        before = None
        for g in range(n_g):
            s2 = [scores((g + 1) * GF + u) for u in range(GF)] if g + 1 < n_g else None
            ps = [soft(g * GF + u, s[u]) for u in range(GF)]
            if before is not None:
                for u in range(GF):
                    mix((g - 1) * GF + u, before[u])
            s, before = s2, ps
        for u in range(GF):
            mix((n_g - 1) * GF + u, before[u])
        return x + nn(owT[l], ms[l, :, tsl])

    def chunk_out(i, t0, w):
        tsl = pl.ds(t0, w)
        pairs = (
            (nq.at[0, :, tsl], nq_hbm.at[:, tsl]), (qs.at[0, :, tsl], qs_hbm.at[:, tsl]),
            (ms.at[0, :, tsl], ms_hbm.at[:, tsl]), (dus.at[0, :, tsl], dus_hbm.at[:, tsl]),
            (probs0.at[:, :, tsl], probs_hbm.at[:, :, tsl]), (invs.at[0, :, tsl], invs_hbm.at[:, tsl]))
        return [pltpu.make_async_copy(a, b, csem.at[k, i]) for k, (a, b) in enumerate(pairs)]

    def chunk_a(i, t0, w, span):
        tsl = pl.ds(t0, w)
        low = pl.multiple_of(t0 // MASKED * SPATIAL // 128 * 128, 128)
        ids = idx_ref[:, tsl] - low
        onehot = (lax.broadcasted_iota(jnp.int32, (span, w), 0) == ids).astype(BF)
        x = wide(gains[3], w) + nn(posT[:, pl.ds(low, span)], onehot)
        x = fwd_layer(0, x, t0, w)
        x = fwd_layer(1, x, t0, w)
        n, r = norm(x, wide(gains[2], w))
        no[:, tsl] = n
        nT = n.T
        e = nn(nT, hw[...]) - err[tsl, :].astype(F32)
        esum[...] += jnp.sum(e * e, axis=0, keepdims=True)
        eb = e.astype(BF)
        err[tsl, :] = eb
        dn = nt(hw[...], eb)
        dx = norm_back(dn, n, r, wide(gains[2], w))
        du = dx.astype(BF)
        dus[1, :, tsl] = du
        attention_back(du, w, tsl, ow.at[1], invs.at[1], ms.at[1], lambda h: probs1[h, :, 0:w], vx.at[1], kT.at[1],
                       qs.at[1], dme, dqs, dkvT)
        dn = nn(qw[1], dqs[:, tsl])
        dx = dx + norm_back(dn, nq[1, :, tsl], rs[1, :, tsl], wide(gains[1], w))
        dus[0, :, tsl] = dx.astype(BF)
        for cp in chunk_out(i, t0, w):
            cp.start()

    full = ROWS // WIDE
    rem = ROWS - full * WIDE
    frames = 1 + -(-(WIDE - 1) // MASKED)

    @pl.loop(0, full)
    def _(i):
        @pl.when(i == 0)
        def _():
            loads[4].wait()
            loads[5].wait()

        chunk_a(i, pl.multiple_of(i * WIDE, WIDE), WIDE, -(-(frames * SPATIAL + 127) // 128) * 128)

    chunk_a(full, full * WIDE, rem, TOKS - full * WIDE // MASKED * SPATIAL // 128 * 128)

    loss_ref[...] = jnp.full((8, 128), jnp.sum(esum[...]), F32)
    emit, finish = make_emit(stage, gsem)
    for b in range(2):
        to = pl.ds(64 * b, 64)
        emit(nn, no[b * 256:(b + 1) * 256, :], lambda c: err[:, c:c + 256], 256, PIX, 48, [
            (0, 40, g1_hbm.at[to, pl.ds(24, 40)]), (40, 48, g2_hbm.at[to, pl.ds(32, 8)])])
    emit(nt, nq[1], lambda c: dqs[c:c + 256, :], DD, DD, 16, [(0, 16, g2_hbm.at[:, pl.ds(0, 16)])])
    emit(nt, ms[1], lambda c: dus[1, c:c + 256, :], DD, DD, 16, [(0, 16, g2_hbm.at[:, pl.ds(16, 16)])])
    dT[0:DD, :] = (dkvT[0:DD, :] * SCALE).astype(BF)
    dT[DD:2 * DD, :] = dkvT[DD:2 * DD, :].astype(BF)
    keep.append(pltpu.make_async_copy(dT, d_hbm, ksem.at[3]))
    keep[3].start()
    for b in range(4):
        to = pl.ds(32 * b, 32)
        emit(nt, nfT[1, b * 352:(b + 1) * 352, :], lambda c: dT[c:c + 256, :], 352, 2 * DD, 88, [
            (0, 64, g0_hbm.at[to, pl.ds(0, 64)]), (64, 88, g1_hbm.at[to, pl.ds(0, 24)])])
    finish()
    for cp in keep:
        cp.wait()

    for i in range(full + 1):
        for cp in chunk_out(i, i * WIDE, min(WIDE, ROWS - i * WIDE)):
            cp.wait()


ROWS_1 = (64, 64, 40)
ROWS_2 = (32, 32, 56)


def compute(features, masked_index, pos_table, mask_token, key_gain, key_weight, query_gain,
            query_weight, out_weight, out_gain, head_weight, target):
    vm = pl.BlockSpec(memory_space=pltpu.VMEM)
    hb = pl.BlockSpec(memory_space=pl.ANY)
    S = jax.ShapeDtypeStruct
    out_shape = (
        S((8, 128), F32), *(S((128, r, 128), F32) for r in ROWS_1),
        S((DD, ROWS), BF), S((DD, ROWS), BF), S((DD, ROWS), BF), S((DD, ROWS), BF),
        S((HEADS, VIS, ROWS), BF), S((HEADS, ROWS), F32),
        S((DD, VIS), BF), S((HEADS, VIS, EXT), BF), S((D, VIS), BF), S((2 * DD, VIS), BF),
    )
    V = pltpu.VMEM
    scratch = [
        V((TOKS, DD), BF), V((2, D, 2 * DD), BF), V((2, DD, DD), BF), V((2, DD, DD), BF), V((DD, PIX), BF),
        V((ROWS, PIX), BF), V((DD, TOKS), BF), V((2, DD, DD), BF), V((2, DD, DD), BF),
        V((2, VIS, D), BF), V((2, D, VIS), BF),
        V((2, HEADS, VIS, 2 * HS), BF), V((2, HEADS, VIS, EXT), BF), V((2, HEADS, EXT, VIS), BF), V((2, DD, VIS), BF),
        V((HEADS, VIS, ROWS), BF), V((HEADS, VIS, WIDE), BF),
        V((2, DD, ROWS), BF), V((2, DD, ROWS), BF), V((2, DD, ROWS), BF), V((2, DD, ROWS), BF), V((DD, ROWS), BF),
        V((DD, ROWS), BF), V((2, 1, ROWS), F32), V((2, HEADS, ROWS), F32), V((2 * DD, VIS), F32),
        V((4, DD, 128), F32), V((HEADS, 2 * HS, WIDE), BF), V((HEADS, EXT, WIDE), BF),
        V((2, SLOT, 128), F32), V((1, PIX), F32), V((2 * DD, VIS), BF),
        pltpu.SemaphoreType.DMA((6,)), pltpu.SemaphoreType.DMA((2, 3)), pltpu.SemaphoreType.DMA((6, NCH)),
        pltpu.SemaphoreType.DMA((4,)),
    ]
    return pl.pallas_call(
        compute_kernel,
        out_shape=out_shape,
        in_specs=[vm] * 6 + [hb] * 6,
        out_specs=[vm] + [hb] * 13,
        scratch_shapes=scratch,
        compiler_params=pltpu.CompilerParams(vmem_limit_bytes=63 * 1024 * 1024),
        name="decode",
    )(
        masked_index, features, mask_token, key_gain, query_gain, out_gain,
        pos_table, key_weight, query_weight, out_weight, head_weight, target,
    )


MESH = pl.DeviceIdType.MESH
PARTS = 3
ORDERS = (("x", "y", "z"), ("y", "z", "x"), ("z", "x", "y"))


def part_index(coords):
    y = coords["y"]
    if isinstance(y, slice):
        return (y, coords["x"], coords["z"], y)
    return (y // 2, coords["x"], coords["z"], y % 2)


def block_shape(free):
    shape = []
    for name, size in (("y", 2), ("x", 4), ("z", 4), ("y", 2)):
        if name in free:
            shape.append(size)
    return tuple(shape)


def reduce_kernel(
    loss_ref, kgain_ref, feat_hbm,
    g0, g1, g2, nq_hbm, qs_hbm, ms_hbm, dus_hbm, probs_hbm, invs_hbm, kT_hbm, vx_hbm, nfT_hbm, d_hbm, ow_hbm, kw_hbm,
    k_out, q_out, o_out, h_out, l_out, fgrad_hbm,
    feat_ref, nq, qs, ms, dus, probs0, invs, kT, vx, nfT, d1, ow, kw, dqs, dkvT, dT, dme, stage, lbuf,
    send, recv, lsem, csem, ksem, gsem, *rest,
):
    own1, own2, got1, got2 = (rest[3 * i:3 * i + 3] for i in range(4))
    buffers = rest[12:]
    clip, tok = lax.axis_index("clip"), lax.axis_index("tok")
    me = {"x": clip % 4, "y": (clip // 4) * 2 + (tok // 2) % 2, "z": tok // 4}
    core = tok % 2
    full_slice = slice(None)

    def device(c, k):
        return ((c["y"] // 2) * 4 + c["x"], c["z"] * 4 + (c["y"] % 2) * 2 + k)

    def shifted(axis, by):
        c = dict(me)
        c[axis] = (me[axis] + by + 4) % 4
        return c

    partner = device(me, 1 - core)
    sides = {a: tuple(device(shifted(a, by), core) for by in (1, -1, 2)) for a in "xyz"}

    chunks = [(i * CH, min(CH, ROWS - i * CH)) for i in range(NCH)]

    def chunk_in(i, t0, w):
        tsl = pl.ds(t0, w)
        pairs = (
            (dus_hbm.at[:, tsl], dus.at[:, tsl]), (invs_hbm.at[:, tsl], invs.at[:, tsl]),
            (ms_hbm.at[:, tsl], ms.at[:, tsl]), (probs_hbm.at[:, :, tsl], probs0.at[:, :, tsl]),
            (qs_hbm.at[:, tsl], qs.at[:, tsl]), (nq_hbm.at[:, tsl], nq.at[:, tsl]))
        return [pltpu.make_async_copy(a, b, csem.at[k, i]) for k, (a, b) in enumerate(pairs)]

    others = [
        pltpu.make_async_copy(ow_hbm.at[0], ow, ksem.at[0]), pltpu.make_async_copy(vx_hbm, vx, ksem.at[1]),
        pltpu.make_async_copy(kT_hbm, kT, ksem.at[2]), pltpu.make_async_copy(nfT_hbm, nfT, ksem.at[3]),
        pltpu.make_async_copy(d_hbm, d1, ksem.at[4]), pltpu.make_async_copy(kw_hbm, kw, ksem.at[5]),
        pltpu.make_async_copy(feat_hbm, feat_ref, ksem.at[6])]
    for cp in others[0:3]:
        cp.start()
    for cp in chunk_in(0, 0, CH):
        cp.start()

    barrier = pltpu.get_barrier_semaphore()
    for dev in [partner] + [d for a in "xyz" for d in sides[a]]:
        pl.semaphore_signal(barrier, inc=1, device_id=dev, device_id_type=MESH)
    pl.semaphore_wait(barrier, 10)

    counter = [0]

    def remote(src, dst, dev):
        i = counter[0]
        counter[0] += 1
        return pltpu.make_async_remote_copy(
            src_ref=src, dst_ref=dst, send_sem=send.at[i], recv_sem=recv.at[i], device_id=dev, device_id_type=MESH)

    class Group:
        def __init__(self, srcs, owns, gots, own_index, bufs, base):
            self.srcs, self.owns, self.gots, self.own_index = srcs, owns, gots, own_index
            self.first, self.second = bufs[0:6], bufs[6:15]
            self.swaps, self.mine = {}, {}
            k = base
            for by in (2, 1, 3, 0):
                for p in range(PARTS):
                    i = part_index(self.coords(p, 0, self.at(p, 0, by)))
                    self.swaps[p, by] = remote(srcs[p].at[i + (1 - core,)], gots[p].at[i], partner)
                    if base is not None:
                        self.mine[p, by] = pltpu.make_async_copy(srcs[p].at[i + (core,)], owns[p].at[i], lsem.at[k])
                        k += 1
            self.far, self.early, self.late, self.direct = {}, {}, {}, {}
            for p in range(PARTS):
                for s in range(2):
                    right, left = sides[ORDERS[p][s]][:2]
                    f, o = self.first[s * 3 + p], self.second[s * 3 + p]
                    lo, hi = self.halves(p, s)
                    self.far[s, p] = (
                        remote(self.block(p, s, 2, lo), f.at[lo], right), remote(self.block(p, s, 2, hi), f.at[hi], left))
                    self.early[s, p] = (
                        remote(self.block(p, s, 1, hi), o.at[0, hi], right),
                        remote(self.block(p, s, 3, lo), o.at[1, lo], left))
                    self.late[s, p] = (
                        remote(self.block(p, s, 1, lo), o.at[0, lo], right),
                        remote(self.block(p, s, 3, hi), o.at[1, hi], left))
                right, left, across = sides[ORDERS[p][2]]
                o = self.second[6 + p]
                self.direct[2, p] = tuple(
                    remote(self.block(p, 2, by), o.at[i], dev) for i, (by, dev) in enumerate(((1, right), (3, left), (2, across))))

        def halves(self, p, s):
            n = block_shape(ORDERS[p][s + 1:])[0]
            return slice(0, n // 2), slice(n // 2, n)

        def at(self, p, s, by):
            return (me[ORDERS[p][s]] + by) % 4

        def coords(self, p, s, j):
            c = {}
            for t, a in enumerate(ORDERS[p]):
                c[a] = me[a] if t < s else (j if t == s else full_slice)
            return c

        def index(self, p, s, by, half=None):
            out = list(part_index(self.coords(p, s, self.at(p, s, by))))
            if half is not None:
                out[[isinstance(i, slice) for i in out].index(True)] = half
            return tuple(out) + self.own_index

        def block(self, p, s, by, half=None):
            return self.owns[p].at[self.index(p, s, by, half)]

        def swap(self, *places):
            for by in places:
                for p in range(PARTS):
                    self.swaps[p, by].start()
                    if self.mine:
                        self.mine[p, by].start()

        def add_swap(self, by):
            for p in range(PARTS):
                if self.mine:
                    self.mine[p, by].wait()
                self.swaps[p, by].wait_recv()

                i = self.index(p, 0, by)
                self.owns[p][i] = self.owns[p][i] + self.gots[p][i[:4]]

        def send_far(self, s):
            for p in range(PARTS):
                for cp in self.far[s, p]:
                    cp.start()

        def send_early(self, s):
            for p in range(PARTS):
                for cp in self.early[s, p]:
                    cp.start()

        def send_late(self, s):
            for p in range(PARTS):
                for cp in self.far[s, p]:
                    cp.wait_recv()
                lo, hi = self.halves(p, s)
                r, l = self.index(p, s, 1, lo), self.index(p, s, 3, hi)
                own, f = self.owns[p], self.first[s * 3 + p]
                own[r] = own[r] + f[lo]
                own[l] = own[l] + f[hi]
                for cp in self.late[s, p]:
                    cp.start()

        def collect(self, s):
            for p in range(PARTS):
                for cp in self.early[s, p] + self.late[s, p]:
                    cp.wait_recv()
                own, o = self.owns[p], self.second[s * 3 + p]
                m = self.index(p, s, 0)
                own[m] = own[m] + o[0] + o[1]

        def send_direct(self):
            for p in range(PARTS):
                for cp in self.direct[2, p]:
                    cp.start()

        def collect_direct(self):
            for p in range(PARTS):
                for cp in self.direct[2, p]:
                    cp.wait_recv()
                own, o = self.owns[p], self.second[6 + p]
                m = self.index(p, 2, 0)
                own[m] = own[m] + o[0] + o[1] + o[2]

        def finish(self):
            for cp in self.swaps.values():
                cp.wait_send()
            for sent in (self.far, self.early, self.late, self.direct):
                for cps in sent.values():
                    for cp in cps:
                        cp.wait_send()

    one = Group((g0, g1, g2), own1, got1, (), buffers[0:15], 0)
    two = Group(own2, own2, got2, (core,), buffers[15:30], None)

    one.swap(2, 1, 3, 0)
    for i, (t0, w) in enumerate(chunks[1:]):
        for cp in chunk_in(i + 1, t0, w):
            cp.start()
    for cp in others[3:]:
        cp.start()
    lbuf[0, core] = loss_ref[...]
    lcopy = remote(loss_ref, lbuf.at[0, core], partner)
    lcopy.start()

    l_near, l_far = [], []
    for s, axis in enumerate("xyz"):
        mine = lbuf.at[s + 1, me[axis]]
        l_near.append([remote(mine, mine, sides[axis][0]), remote(mine, mine, sides[axis][1])])
        far = lbuf.at[s + 1, (me[axis] + 3) % 4]
        l_far.append(remote(far, far, sides[axis][0]))

    def loss_near(s):
        if s == 0:
            lcopy.wait()
            tile = lbuf[0, 0] + lbuf[0, 1]
        else:
            l_far[s - 1].wait()
            tile = lbuf[s, 0] + lbuf[s, 1] + lbuf[s, 2] + lbuf[s, 3]
        lbuf[s + 1, me["xyz"[s]]] = tile
        for cp in l_near[s]:
            cp.start()

    def loss_far(s):
        for cp in l_near[s]:
            cp.wait()
        l_far[s].start()

    dkvT[...] = jnp.zeros_like(dkvT)
    for cp in others[0:3]:
        cp.wait()

    def chunk_b(i, t0, w):
        tsl = pl.ds(t0, w)
        for cp in chunk_in(i, t0, w):
            cp.wait()
        attention_back(dus[:, tsl], w, tsl, ow, invs, ms, lambda h: probs0[h, :, tsl], vx, kT, qs, dme, dqs, dkvT)

    @pl.loop(0, ROWS // CH)
    def _(i):
        chunk_b(i, pl.multiple_of(i * CH, CH), CH)

        @pl.when(i == 1)
        def _():
            one.add_swap(2)
            one.send_far(0)
            loss_near(0)

        @pl.when(i == 3)
        def _():
            one.add_swap(1)
            one.add_swap(3)
            one.send_early(0)

    chunk_b(NCH - 1, *chunks[NCH - 1])
    one.send_late(0)
    loss_far(0)

    emit, flush = make_emit(stage, gsem)
    flat = [o.reshape(128, r, 128) for o, r in zip(own2, ROWS_2)]
    emit(nt, nq[...], lambda c: dqs[c:c + 256, :], DD, DD, 16, [(0, 16, flat[2].at[:, pl.ds(24, 16)])])
    emit(nt, ms[...], lambda c: dus[c:c + 256, :], DD, DD, 16, [(0, 16, flat[2].at[:, pl.ds(40, 16)])])
    dT[0:DD, :] = (dkvT[0:DD, :] * SCALE).astype(BF)
    dT[DD:2 * DD, :] = dkvT[DD:2 * DD, :].astype(BF)
    others[3].wait()
    for b in range(4):
        to = pl.ds(32 * b, 32)
        emit(nt, nfT[b * 352:(b + 1) * 352, :], lambda c: dT[c:c + 256, :], 352, 2 * DD, 88, [
            (0, 32, flat[0].at[to]), (32, 64, flat[1].at[to]), (64, 88, flat[2].at[to, pl.ds(0, 24)])])
    flush()
    two.swap(2, 1, 3, 0)

    def feature_grad(l, d):
        dn = nt(d.T, kw[l])
        xh, r = feature_norm(feat_ref, l)
        dxh = dn * kgain_ref[l:l + 1, :].astype(F32)
        m1 = jnp.mean(dxh, axis=1, keepdims=True)
        m2 = jnp.mean(dxh * xh, axis=1, keepdims=True)
        feat_ref[l] = (r * (dxh - m1 - xh * m2)).astype(BF)

    for cp in others[4:]:
        cp.wait()
    two.add_swap(2)
    two.send_far(0)
    two.add_swap(1)
    two.add_swap(3)
    two.send_early(0)
    one.add_swap(0)
    one.collect(0)
    one.send_far(1)
    one.send_early(1)
    loss_near(1)
    feature_grad(0, dT[...])
    feature_grad(1, d1[...])
    f_copy = pltpu.make_async_copy(feat_ref, fgrad_hbm, ksem.at[7])
    f_copy.start()
    two.add_swap(0)
    two.send_late(0)
    one.send_late(1)
    loss_far(1)
    one.collect(1)
    one.send_direct()
    loss_near(2)
    two.collect(0)
    two.send_far(1)
    two.send_early(1)
    loss_far(2)
    one.collect_direct()
    two.send_late(1)
    l_far[2].wait()
    l_out[...] = lbuf[3, 0] + lbuf[3, 1] + lbuf[3, 2] + lbuf[3, 3]
    two.collect(1)
    two.send_direct()

    at = part_index(me)

    def rows(group, p, start, n, stride=1):
        own = own1 if group == 1 else own2
        ix = at if group == 1 else at + (core,)
        return own[p][ix + ((pl.ds(start, n, stride=stride)),)] if stride > 1 else own[p][ix + (pl.ds(start, n),)]

    for j in range(8):
        k_out[1, 0:8, j * 128:(j + 1) * 128] = rows(1, 0, j, 8, 8)
        k_out[1, 8:11, j * 128:(j + 1) * 128] = rows(1, 1, j, 3, 8)
    for j in range(4):
        q_out[1, :, j * 128:(j + 1) * 128] = rows(1, 2, j, 4, 4)
        o_out[1, :, j * 128:(j + 1) * 128] = rows(1, 2, 16 + j, 4, 4)
    for r in range(4):
        for j in range(12):
            i = r * 12 + j
            h_out[r:r + 1, j * 128:(j + 1) * 128] = rows(1, 1, 24 + i, 1) if i < 40 else rows(1, 2, i - 8, 1)
    two.collect_direct()
    for j in range(8):
        lanes = slice(j * 128, (j + 1) * 128)
        k_out[0, 0:4, lanes] = rows(2, 0, j, 4, 8)
        k_out[0, 4:8, lanes] = rows(2, 1, j, 4, 8)
        k_out[0, 8:11, lanes] = rows(2, 2, j, 3, 8)
    for j in range(4):
        lanes = slice(j * 128, (j + 1) * 128)
        q_out[0, :, lanes] = rows(2, 2, 24 + j, 4, 4)
        o_out[0, :, lanes] = rows(2, 2, 40 + j, 4, 4)
    one.finish()
    two.finish()
    f_copy.wait()


def reduce_scatter(state, features, key_gain, key_weight, out_weight):
    V = pltpu.VMEM
    vm = pl.BlockSpec(memory_space=pltpu.VMEM)
    hb = pl.BlockSpec(memory_space=pl.ANY)
    S = jax.ShapeDtypeStruct
    loss, parts, rest = state[0], state[1:4], state[4:]
    grid = (2, 4, 4, 2)
    scratch = [
        V((2, VIS, D), BF),
        V((DD, ROWS), BF), V((DD, ROWS), BF), V((DD, ROWS), BF), V((DD, ROWS), BF),
        V((HEADS, VIS, ROWS), BF), V((HEADS, ROWS), F32),
        V((DD, VIS), BF), V((HEADS, VIS, EXT), BF), V((D, VIS), BF), V((2 * DD, VIS), BF),
        V((DD, DD), BF), V((2, D, 2 * DD), BF), V((DD, ROWS), BF), V((2 * DD, VIS), F32), V((2 * DD, VIS), BF),
        V((HEADS, EXT, CH), BF), V((2, SLOT, 128), F32), V((4, 4, 8, 128), F32),
    ]
    n_copies = 2 * (12 + 36 + 9) + 1 + 9
    dma = pltpu.SemaphoreType.DMA
    scratch += [dma((n_copies,)), dma((n_copies,)), dma((12,)), dma((6, NCH)), dma((8,)), dma((2, 3))]
    scratch += [V(grid + (r, 128), F32) for r in ROWS_1] + [V(grid + (2, r, 128), F32) for r in ROWS_2]
    scratch += [V(grid + (r, 128), F32) for r in ROWS_1] + [V(grid + (r, 128), F32) for r in ROWS_2]
    for rows in (ROWS_1, ROWS_2):
        for n, stages in (((), (0, 1)), ((2,), (0, 1)), ((3,), (2,))):
            for s in stages:
                for p in range(PARTS):
                    scratch.append(V(n + block_shape(ORDERS[p][s + 1:]) + (rows[p], 128), F32))
    return pl.pallas_call(
        reduce_kernel,
        out_shape=(
            S((2, 11, 2 * DD), F32), S((2, 4, DD), F32), S((2, 4, DD), F32), S((4, PIX), F32), S((8, 128), F32),
            S((2, VIS, D), BF),
        ),
        in_specs=[vm] * 2 + [hb] * 16,
        out_specs=[vm] * 5 + [hb],
        scratch_shapes=scratch,
        compiler_params=pltpu.CompilerParams(
            collective_id=0, has_side_effects=True, vmem_limit_bytes=63 * 1024 * 1024),
        name="reduce",
    )(
        loss, key_gain, features, *(g.reshape(grid + (2,) + g.shape[1:]) for g in parts), *rest, out_weight, key_weight)


def output_kernel(loss, k_in, q_in, o_in, h_in, f_in, loss_out, k_out, q_out, o_out, h_out, f_out):
    loss_out[0, 0] = loss[0, 0] * (1.0 / (128 * ROWS * PIX))
    for l in range(2):
        k_out[:, l, :] = k_in[l]
    for a, b in ((f_in, f_out), (q_in, q_out), (o_in, o_out), (h_in, h_out)):
        b[...] = a[...]


def outputs(k, q, o, h, loss, f):
    vm = pl.BlockSpec(memory_space=pltpu.VMEM)
    sm = pl.BlockSpec(memory_space=pltpu.SMEM)
    arrays = (k, q, o, h, f)
    return pl.pallas_call(
        output_kernel,
        out_shape=(jax.ShapeDtypeStruct((1, 1), F32), jax.ShapeDtypeStruct((11, 2, 2 * DD), F32),
                   *(jax.ShapeDtypeStruct(a.shape, a.dtype) for a in arrays[1:])),
        in_specs=[sm] + [vm] * 5,
        out_specs=[sm] + [vm] * 5,
        name="outputs",
    )(loss, *arrays)


def shards(features, masked_index, pos_table, mask_token, key_gain, key_weight, query_gain,
           query_weight, out_weight, out_gain, head_weight, target):
    state = compute(
        features, masked_index, pos_table, mask_token, key_gain, key_weight, query_gain,
        query_weight, out_weight, out_gain, head_weight, target)
    summed = reduce_scatter(state, features, key_gain, key_weight, out_weight)
    loss, key_grad, query_grad, out_grad, head_grad, feature_grad = outputs(*summed)
    return loss[0, 0], feature_grad, key_grad.transpose(1, 0, 2), query_grad, out_grad, head_grad


def solution(mesh):
    both = ("clip", "tok")
    in_specs = (
        P(None, both, None), P(both, None), P(), P(), P(), P(), P(), P(), P(), P(), P(), P(both, None, None))
    out_specs = (
        P(), P(None, both, None), P(None, both, None), P(None, both, None), P(None, both, None), P(both, None))
    return jax.shard_map(shards, mesh=mesh, in_specs=in_specs, out_specs=out_specs, check_vma=False)
```
